32 devices in a mesh: tm: 8 (over z, core), pts: 4 (over y, x).
Axes of the slice: x: 2, y: 2, z: 4, core: 2. Of those that a mesh axis runs over, the one named last changes fastest.
Arguments:
- snapshots: float32 [1024, 16384], P('tm', 'pts'), may hold values from -110 to 110
- weights: float32 [16384], P(('pts', 'tm')), may hold values from 0.25 to 12, as said below
Outputs:
- modes: float32 [2, 33, 31, 16384], P(None, None, None, ('pts', 'tm'))
- triangle: float32 [2, 33, 31, 31], replicated
The draws below stay inside these ranges and needn't reach their ends.
Inputs may be any that keep to these rules, and one draw needn't show every extreme that they name: Positive weights.
All inputs are finite; a program needn't handle non-finite values.
Results may differ from the reference program's by a relative error of at most 0.00065.
Values sent between devices are 32-bit elements; how exact they have to be, the bound alone decides.
No kernel may reach another device: no remote copies, remote signals or barrier semaphores. Data moves between devices by JAX's collectives and lax.ppermute only.
A program may use at most 128 MiB of HBM per device.

```python
import math
import jax
import jax.numpy as jnp
from jax import lax

SEG = 64
HOP = 32
NF = 33
NT = 1024
NB = 31
NP = 16384


def draw_snapshots(key, part):
    key_noise, key_time, key_point, key_coef, key_shape = jax.random.split(key, 5)
    noise_level = 0.0004 * math.sqrt(NB)
    coefficient = jnp.clip(jax.random.normal(key_coef, (NT, 8), jnp.float32), -2.5, 2.5)
    pattern = jnp.clip(jax.random.normal(key_shape, (8, NP), jnp.float32), -2.5, 2.5)
    noise_part = jnp.clip(jax.random.normal(key_noise, (NT, NP), jnp.float32), -4.0, 4.0)
    time_scale = jnp.exp(jax.random.uniform(key_time, (NT, 1), jnp.float32, math.log(0.5), math.log(2.0)))
    point_scale = jnp.exp(jax.random.uniform(key_point, (1, NP), jnp.float32, 0.0, math.log(10.0)))
    values = jnp.zeros((NT, NP), jnp.float32)
    for mode_number in range(8):
        amplitude = 0.25 * math.exp(-math.log(10.0) * mode_number / 7.0)
        values = values + amplitude * coefficient[:, mode_number:mode_number + 1] * pattern[mode_number:mode_number + 1, :]
    values = (values + noise_level * noise_part) * time_scale * point_scale
    return values.astype(jnp.float32)


def draw_weights(key, part):
    trend = 1.0 + 2.0 * jnp.arange(NP).astype(jnp.float32) / NP
    rough = jnp.exp(jax.random.uniform(key, (NP,), jnp.float32, math.log(0.5), math.log(2.0)))
    return (trend * rough).astype(jnp.float32)


def setup_inputs(seed: int = 0) -> dict:
    streams_of = jax.random.split(jax.random.key(seed), 3)
    return {
        "snapshots": draw_snapshots(jax.random.fold_in(streams_of[2], 71), 0),
        "weights": draw_weights(jax.random.fold_in(streams_of[2], 71), 0),
    }


EXACT = lax.Precision.HIGHEST

def fourier_table():
    sample = jnp.arange(SEG).astype(jnp.float32)[:, None]
    column = jnp.arange(SEG)[None, :]
    frequency = jnp.where(column < NF, column, column - HOP).astype(jnp.float32)
    window = 0.5 - 0.5 * jnp.cos(2.0 * math.pi * sample / SEG)
    phase_angle = 2.0 * math.pi * frequency * sample / SEG
    waveform = jnp.where(column < NF, jnp.cos(phase_angle), -jnp.sin(phase_angle))
    return waveform * window / jnp.sqrt(jnp.float32(3 * SEG / 8))

def split_spectrum(spectrum):
    padding = jnp.zeros((1,) + spectrum.shape[1:], spectrum.dtype)
    part_real = spectrum[:NF]
    part_imag = jnp.concatenate([padding, spectrum[NF:], padding], axis=0)
    return (part_real, part_imag)

def gram(left_real, left_imag):

    def contract(first, second):
        return jnp.einsum('fbp,fcp->fbc', first, second, precision=EXACT)
    return (contract(left_real, left_real) + contract(left_imag, left_imag), contract(left_real, left_imag) - contract(left_imag, left_real))

def cholesky_upper(gram_real, gram_imag):
    width = gram_real.shape[-1]
    position = jnp.arange(width)

    def advance(k, loop_state):
        work_real, work_imag, upper_real, upper_imag = loop_state
        pivot_real = lax.dynamic_index_in_dim(work_real, k, axis=1, keepdims=False)
        pivot_imag = lax.dynamic_index_in_dim(work_imag, k, axis=1, keepdims=False)
        pivot = jnp.sqrt(lax.dynamic_index_in_dim(pivot_real, k, axis=1, keepdims=False))
        keep_mask = (position >= k)[None, :]
        pivot_real = jnp.where(keep_mask, pivot_real / pivot[:, None], 0.0)
        pivot_imag = jnp.where(keep_mask, pivot_imag / pivot[:, None], 0.0)
        upper_real = lax.dynamic_update_index_in_dim(upper_real, pivot_real, k, axis=1)
        upper_imag = lax.dynamic_update_index_in_dim(upper_imag, pivot_imag, k, axis=1)
        work_real = work_real - (pivot_real[:, :, None] * pivot_real[:, None, :] + pivot_imag[:, :, None] * pivot_imag[:, None, :])
        work_imag = work_imag - (pivot_real[:, :, None] * pivot_imag[:, None, :] - pivot_imag[:, :, None] * pivot_real[:, None, :])
        return (work_real, work_imag, upper_real, upper_imag)
    start = (gram_real, gram_imag, jnp.zeros_like(gram_real), jnp.zeros_like(gram_imag))
    result = lax.fori_loop(0, width, advance, start)
    return (result[2], result[3])

def invert_upper(upper_real, upper_imag):
    width = upper_real.shape[-1]
    position = jnp.arange(width)

    def advance(i, loop_state):
        inverse_real, inverse_imag = loop_state
        k = width - 1 - i
        row_real = lax.dynamic_index_in_dim(upper_real, k, axis=1, keepdims=False)
        row_imag = lax.dynamic_index_in_dim(upper_imag, k, axis=1, keepdims=False)
        pivot = lax.dynamic_index_in_dim(row_real, k, axis=1, keepdims=False)

        def contract(first, second):
            return jnp.einsum('fj,fjc->fc', first, second, precision=EXACT)
        sum_real = contract(row_real, inverse_real) - contract(row_imag, inverse_imag)
        sum_imag = contract(row_real, inverse_imag) + contract(row_imag, inverse_real)
        unit_row = (position == k).astype(upper_real.dtype)[None, :]
        new_real = (unit_row - sum_real) / pivot[:, None]
        new_imag = -sum_imag / pivot[:, None]
        inverse_real = lax.dynamic_update_index_in_dim(inverse_real, new_real, k, axis=1)
        inverse_imag = lax.dynamic_update_index_in_dim(inverse_imag, new_imag, k, axis=1)
        return (inverse_real, inverse_imag)
    return lax.fori_loop(0, width, advance, (jnp.zeros_like(upper_real), jnp.zeros_like(upper_imag)))

def apply_inverse(basis_real, basis_imag, inverse_real, inverse_imag):

    def contract(first, second):
        return jnp.einsum('fbc,fbp->fcp', first, second, precision=EXACT)
    return (contract(inverse_real, basis_real) - contract(inverse_imag, basis_imag), contract(inverse_real, basis_imag) + contract(inverse_imag, basis_real))

def product_upper(left_real, left_imag, right_real, right_imag):

    def contract(first, second):
        return jnp.einsum('fbj,fjc->fbc', first, second, precision=EXACT)
    return (contract(left_real, right_real) - contract(left_imag, right_imag), contract(left_real, right_imag) + contract(left_imag, right_real))

def factorize(basis_real, basis_imag):
    gram_real, gram_imag = gram(basis_real, basis_imag)
    upper_real, upper_imag = cholesky_upper(gram_real / NP, gram_imag / NP)
    inverse_real, inverse_imag = invert_upper(upper_real, upper_imag)
    ortho_real, ortho_imag = apply_inverse(basis_real, basis_imag, inverse_real, inverse_imag)
    return (ortho_real, ortho_imag, upper_real, upper_imag)

def reference(snapshots, weights):
    hop_rows = snapshots.reshape(NT // HOP, HOP, snapshots.shape[1])
    blocks = jnp.concatenate([hop_rows[:-1], hop_rows[1:]], axis=1)
    spectrum = jnp.einsum('bnp,nc->cbp', blocks, fourier_table(), precision=EXACT)
    part_real, part_imag = split_spectrum(spectrum)
    root_weight = jnp.sqrt(weights)[None, None, :]
    first_real, first_imag, upper1_real, upper1_imag = factorize(part_real * root_weight, part_imag * root_weight)
    final_real, final_imag, upper2_real, upper2_imag = factorize(first_real, first_imag)
    total_real, total_imag = product_upper(upper2_real, upper2_imag, upper1_real, upper1_imag)
    return (jnp.stack([final_real, final_imag]), jnp.stack([total_real, total_imag]))
```

```python
import functools
import math

import jax
import jax.numpy as jnp
import numpy as np
from jax import lax
from jax.experimental import pallas as pl
from jax.experimental.pallas import tpu as pltpu
from jax.sharding import PartitionSpec as P

SEG = 64
HOP = 32
NF = 33
NT = 1024
NB = 31
SLOTS = 32
GROUPS = 8
VMEM_BYTES = 40 * 1024 * 1024


def fourier_table():
    sample = np.arange(SEG, dtype=np.float64)[:, None]
    column = np.arange(SEG)[None, :]
    frequency = np.where(column < NF, column, column - HOP).astype(np.float64)
    window = 0.5 - 0.5 * np.cos(2.0 * math.pi * sample / SEG)
    phase_angle = 2.0 * math.pi * frequency * sample / SEG
    waveform = np.where(column < NF, np.cos(phase_angle), -np.sin(phase_angle))
    return (waveform * window / math.sqrt(3 * SEG / 8)).astype(np.float32)


def slices_of(value, count):
    parts = []
    for number in range(count):
        part = value.astype(jnp.bfloat16)
        parts.append(part)
        if number + 1 < count:
            value = value - part.astype(jnp.float32)
    return parts


def spectrum_body(table_t, records, spec_ref):
    t1, t2, t3 = slices_of(table_t, 3)
    left = jnp.concatenate([t1, t1, t1, t2, t2, t3], axis=1)
    x1, x2, x3 = slices_of(records, 3)
    points = records.shape[1]
    for b in range(NB):
        at = slice(HOP * b, HOP * b + SEG)
        right = jnp.concatenate([x1[at], x2[at], x3[at], x1[at], x2[at], x1[at]], axis=0)
        spec_ref[:, b, :] = jnp.dot(left, right, preferred_element_type=jnp.float32)
    spec_ref[:, NB, :] = jnp.zeros((SEG, points), jnp.float32)


def gram_body(real_of, imag_of, gram_ref, count):
    for g in range(GROUPS):
        reals, imags = [], []
        for s in range(4):
            slot = 4 * g + s
            real = slices_of(real_of(slot), count)
            imag = slices_of(imag_of(slot), count)
            left = [jnp.concatenate([r, i], axis=1) for r, i in zip(real, imag)]
            right = []
            for r, i in zip(real, imag):
                if slot == 0:
                    zero = jnp.zeros_like(r)
                    right.append(jnp.concatenate([r, zero], axis=1))
                    right.append(jnp.concatenate([zero, i], axis=1))
                else:
                    right.append(jnp.concatenate([r, i], axis=1))
                    right.append(jnp.concatenate([i, -r], axis=1))
            products = lax.dot_general(
                jnp.concatenate(left, axis=0),
                jnp.concatenate(right, axis=0),
                (((1,), (1,)), ((), ())),
                preferred_element_type=jnp.float32,
            )
            total = None
            for order in reversed(range(2 * count - 1)):
                for row in range(count):
                    column = order - row
                    if 0 <= column < count:
                        part = products[32 * row:32 * row + 32, 64 * column:64 * column + 64]
                        total = part if total is None else total + part
            reals.append(total[:, :32])
            imags.append(total[:, 32:])
        gram_ref[0, :, g, :] = jnp.concatenate(reals, axis=1)
        gram_ref[1, :, g, :] = jnp.concatenate(imags, axis=1)


def apply_group(lower_ref, g, reals, imags, count):
    lane = lax.broadcasted_iota(jnp.int32, (32, 128), 1) // 32
    lower_real, lower_imag = lower_ref[0, :, g, :], lower_ref[1, :, g, :]
    rows = []
    for s in range(4):
        mine = lane == s
        own_real = jnp.where(mine, lower_real, 0.0)
        own_imag = jnp.where(mine, lower_imag, 0.0)
        if g == 0 and s == 0:
            zero = jnp.zeros_like(own_real)
            rows.append(jnp.concatenate([own_real, zero], axis=1))
            rows.append(jnp.concatenate([zero, own_imag], axis=1))
        else:
            rows.append(jnp.concatenate([own_real, own_imag], axis=1))
            rows.append(jnp.concatenate([-own_imag, own_real], axis=1))
    left = slices_of(jnp.concatenate(rows, axis=0), count)
    right = slices_of(jnp.concatenate([reals, imags], axis=0), count)
    total = None
    for order in reversed(range(count)):
        for row in range(order + 1):
            part = jnp.dot(left[row], right[order - row], preferred_element_type=jnp.float32)
            total = part if total is None else total + part
    return total


def factor_body(gram, scale, upper_ref, lower_ref, save_ref):
    shape = (GROUPS, 128)
    lane = lax.broadcasted_iota(jnp.int32, shape, 1)
    column = lane % 32
    base = lane - column
    pair = jnp.logical_and(lane < 32, lax.broadcasted_iota(jnp.int32, shape, 0) == 0)
    zero = jnp.zeros(shape, jnp.float32)

    def spread(value, at):
        return jnp.take_along_axis(value, base + at, axis=1, mode="promise_in_bounds")

    done = []
    for i in range(NB):
        work_real = jnp.where(column >= i, gram(0, i) * scale, 0.0)
        work_imag = jnp.where(column >= i, gram(1, i) * scale, 0.0)
        for k in range(i):
            row_real, row_imag = save_ref[0, k], save_ref[1, k]
            pick_real = spread(row_real, i)
            pick_imag = spread(row_imag, i)
            cross = jnp.where(pair, 0.0, pick_imag)
            own = jnp.where(pair, pick_imag, pick_real)
            here = column == k
            work_real = jnp.where(here, 0.0, work_real) - (pick_real * row_real + cross * row_imag)
            work_imag = jnp.where(here, 0.0, work_imag) - (own * row_imag - cross * row_real)
        pivot_real = spread(work_real, i)
        pivot_imag = jnp.where(pair, spread(work_imag, i), pivot_real)
        root_real, root_imag = jnp.sqrt(pivot_real), jnp.sqrt(pivot_imag)
        inverse_real, inverse_imag = 1.0 / root_real, 1.0 / root_imag
        here = column == i
        row_real = work_real * inverse_real
        row_imag = work_imag * inverse_imag
        diag_imag = jnp.where(pair, root_imag, 0.0)
        upper_ref[0, i] = jnp.where(column > i, row_real, jnp.where(here, root_real, 0.0))
        upper_ref[1, i] = jnp.where(column > i, row_imag, jnp.where(here, diag_imag, 0.0))
        row_real = jnp.where(here, inverse_real, row_real)
        row_imag = jnp.where(here, jnp.where(pair, inverse_imag, 0.0), row_imag)
        save_ref[0, i] = row_real
        save_ref[1, i] = row_imag
        lower_ref[0, i] = jnp.where(column <= i, row_real, 0.0)
        lower_ref[1, i] = jnp.where(column <= i, row_imag, 0.0)
    for part in range(2):
        upper_ref[part, NB] = zero
        lower_ref[part, NB] = zero


def spectrum_kernel(me_ref, table_ref, root_ref, *refs, tm, count):
    pieces, (spec_ref, gram_ref, records_ref) = refs[:tm], refs[tm:]
    rows = pieces[0].shape[0]
    root = root_ref[...]
    for d in range(tm):
        start = pl.multiple_of((me_ref[0] ^ d) * rows, rows)
        records_ref[pl.ds(start, rows), :] = pieces[d][...] * root
    spectrum_body(table_ref[...], records_ref[...], spec_ref)
    gram_body(lambda slot: spec_ref[slot], lambda slot: spec_ref[SLOTS + slot], gram_ref, count)


def gather_gram(place_ref, pieces, whole_ref):
    for c in range(2):
        for d in range(len(pieces[c])):
            piece = pieces[c][d]
            rows = piece.shape[0]
            start = pl.multiple_of((place_ref[1] ^ d) * rows, rows)
            whole_ref[place_ref[0] ^ c, pl.ds(start, rows)] = piece[...]


def factor_kernel(place_ref, *refs, pts, scale):
    pieces = refs[:pts], refs[pts:2 * pts]
    upper_ref, lower_ref, whole_ref, save_ref = refs[2 * pts:]
    gather_gram(place_ref, pieces, whole_ref)
    factor_body(lambda part, i: whole_ref[part, i], scale, upper_ref, lower_ref, save_ref)


def second_factor_kernel(place_ref, *refs, pts, scale):
    pieces = refs[:pts], refs[pts:2 * pts]
    first_ref, triangle_ref, lower_ref, whole_ref, save_ref, upper_ref = refs[2 * pts:]
    gather_gram(place_ref, pieces, whole_ref)
    factor_body(lambda part, i: whole_ref[part, i], scale, upper_ref, lower_ref, save_ref)
    shape = (GROUPS, 128)
    lane = lax.broadcasted_iota(jnp.int32, shape, 1)
    base = lane - lane % 32
    pair = jnp.logical_and(lane < 32, lax.broadcasted_iota(jnp.int32, shape, 0) == 0)
    for i in range(NB):
        row_real, row_imag = upper_ref[0, i], upper_ref[1, i]
        total_real = total_imag = None
        for k in range(i, NB):
            pick_real = jnp.take_along_axis(row_real, base + k, axis=1, mode="promise_in_bounds")
            pick_imag = jnp.take_along_axis(row_imag, base + k, axis=1, mode="promise_in_bounds")
            cross = jnp.where(pair, 0.0, pick_imag)
            own = jnp.where(pair, pick_imag, pick_real)
            other_real, other_imag = first_ref[0, k], first_ref[1, k]
            part_real = pick_real * other_real - cross * other_imag
            part_imag = own * other_imag + cross * other_real
            total_real = part_real if total_real is None else total_real + part_real
            total_imag = part_imag if total_imag is None else total_imag + part_imag
        whole_ref[0, i] = total_real
        whole_ref[1, i] = total_imag
    for g in range(GROUPS):
        real, imag = whole_ref[0, :, g, :], whole_ref[1, :, g, :]
        for s in range(4):
            triangle_ref[0, 4 * g + s] = real[:NB, 32 * s:32 * s + NB]
            triangle_ref[1, 4 * g + s] = imag[:NB, 32 * s:32 * s + NB]
            if g == 0 and s == 0:
                triangle_ref[0, SLOTS] = imag[:NB, :NB]
                triangle_ref[1, 0] = jnp.zeros((NB, NB), jnp.float32)
                triangle_ref[1, SLOTS] = jnp.zeros((NB, NB), jnp.float32)


def first_apply_kernel(lower_ref, spec_ref, ortho_ref, gram_ref, *, apply_count, gram_count):
    points = spec_ref.shape[-1]
    for g in range(GROUPS):
        reals = spec_ref[4 * g:4 * g + 4].reshape(128, points)
        imags = spec_ref[SLOTS + 4 * g:SLOTS + 4 * g + 4].reshape(128, points)
        out = apply_group(lower_ref, g, reals, imags, apply_count)
        for s in range(4):
            ortho_ref[4 * g + s] = out[64 * s:64 * s + 32]
            ortho_ref[SLOTS + 4 * g + s] = out[64 * s + 32:64 * s + 64]
    gram_body(lambda slot: ortho_ref[slot], lambda slot: ortho_ref[SLOTS + slot], gram_ref, gram_count)


def last_apply_kernel(lower_ref, ortho_ref, modes_ref, *, apply_count):
    points = ortho_ref.shape[-1]
    zero = jnp.zeros((NB, points), jnp.float32)
    modes_ref[1, 0] = zero
    modes_ref[1, SLOTS] = zero
    for g in range(GROUPS):
        reals = ortho_ref[4 * g:4 * g + 4].reshape(128, points)
        imags = ortho_ref[SLOTS + 4 * g:SLOTS + 4 * g + 4].reshape(128, points)
        out = apply_group(lower_ref, g, reals, imags, apply_count)
        for s in range(4):
            slot = 4 * g + s
            modes_ref[0, slot] = out[64 * s:64 * s + NB]
            if slot == 0:
                modes_ref[0, SLOTS] = out[32:32 + NB]
            else:
                modes_ref[1, slot] = out[64 * s + 32:64 * s + 32 + NB]


def call(body, out_shape, scratch, in_smem, operands):
    smem = pl.BlockSpec(memory_space=pltpu.SMEM)
    vmem = pl.BlockSpec(memory_space=pltpu.VMEM)
    return pl.pallas_call(
        body,
        out_shape=out_shape,
        in_specs=[smem] * in_smem + [vmem] * (len(operands) - in_smem),
        out_specs=jax.tree.map(lambda _: vmem, out_shape),
        scratch_shapes=scratch,
        compiler_params=pltpu.CompilerParams(vmem_limit_bytes=VMEM_BYTES),
    )(*operands)


def f32(*shape):
    return jax.ShapeDtypeStruct(shape, jnp.float32)


def xor_pairs(size, difference):
    return [(i, i ^ difference) for i in range(size)]


def tree_sum(values):
    while len(values) > 1:
        values = [values[i] + values[i + 1] for i in range(0, len(values), 2)]
    return values[0]


def sum_over_devices(gram):
    tm, pts = lax.axis_size("tm"), lax.axis_size("pts")
    core, here = lax.axis_index("tm") & 1, lax.axis_index("pts")
    mine = lax.dynamic_index_in_dim(gram, core, 0, keepdims=False)
    theirs = lax.dynamic_index_in_dim(gram, 1 - core, 0, keepdims=False)
    half = mine + lax.ppermute(theirs, "tm", xor_pairs(tm, 1))
    rows = 32 // pts
    parts = []
    for d in range(pts):
        part = lax.dynamic_slice_in_dim(half, (here ^ d) * rows, rows, 0)
        parts.append(part if d == 0 else lax.ppermute(part, "pts", xor_pairs(pts, d)))
    part = tree_sum(parts)
    part = tree_sum([part] + [lax.ppermute(part, "tm", xor_pairs(tm, 2 * d)) for d in range(1, tm // 2)])
    own = [part] + [lax.ppermute(part, "pts", xor_pairs(pts, d)) for d in range(1, pts)]
    return own + [lax.ppermute(piece, "tm", xor_pairs(tm, 1)) for piece in own]


def shards(snapshots, weights):
    tm, pts = lax.axis_size("tm"), lax.axis_size("pts")
    me = lax.axis_index("tm")
    rows, points = snapshots.shape[0], weights.shape[0]
    scale = 1.0 / (points * tm * pts)
    pieces = []
    for d in range(tm):
        piece = lax.dynamic_slice_in_dim(snapshots, (me ^ d) * points, points, 1)
        pieces.append(piece if d == 0 else lax.ppermute(piece, "tm", xor_pairs(tm, d)))
    root = jnp.sqrt(weights)[None, :]
    table_t = jnp.asarray(fourier_table().T)
    square = f32(2, 32, GROUPS, 128)
    square_scratch = pltpu.VMEM((2, 32, GROUPS, 128), jnp.float32)
    place = jnp.stack([me & 1, lax.axis_index("pts")]).astype(jnp.int32)

    spec, gram = call(
        functools.partial(spectrum_kernel, tm=tm, count=3),
        (f32(SEG, 32, points), square),
        [pltpu.VMEM((NT, points), jnp.float32)],
        1,
        [me[None].astype(jnp.int32), table_t, root] + pieces,
    )
    upper1, lower1 = call(
        functools.partial(factor_kernel, pts=pts, scale=scale),
        (square, square),
        [square_scratch] * 2,
        1,
        [place] + sum_over_devices(gram),
    )
    ortho, gram2 = call(
        functools.partial(first_apply_kernel, apply_count=3, gram_count=2),
        (f32(SEG, 32, points), square),
        [],
        0,
        [lower1, spec],
    )
    triangle, lower2 = call(
        functools.partial(second_factor_kernel, pts=pts, scale=scale),
        (f32(2, NF, NB, NB), square),
        [square_scratch] * 3,
        1,
        [place] + sum_over_devices(gram2) + [upper1],
    )
    modes = call(
        functools.partial(last_apply_kernel, apply_count=2),
        f32(2, NF, NB, points),
        [],
        0,
        [lower2, ortho],
    )
    return (modes, triangle)


def solution(mesh):
    placed = (P("tm", "pts"), P(("pts", "tm")))
    return jax.shard_map(
        shards,
        mesh=mesh,
        in_specs=placed,
        out_specs=(P(None, None, None, ("pts", "tm")), P()),
        check_vma=False,
    )
```

```python
import functools
import math

import jax
import jax.numpy as jnp
import numpy as np
from jax import lax
from jax.experimental import pallas as pl
from jax.experimental.pallas import tpu as pltpu
from jax.sharding import PartitionSpec as P

SEG = 64
HOP = 32
NF = 33
NT = 1024
NB = 31
SLOTS = 32
GROUPS = 8
SIDE = 4
CUTS = 4
VMEM_BYTES = 24 * 1024 * 1024


def fourier_table():
    sample = np.arange(SEG, dtype=np.float64)[:, None]
    column = np.arange(SEG)[None, :]
    frequency = np.where(column < NF, column, column - HOP).astype(np.float64)
    window = 0.5 - 0.5 * np.cos(2.0 * math.pi * sample / SEG)
    phase_angle = 2.0 * math.pi * frequency * sample / SEG
    waveform = np.where(column < NF, np.cos(phase_angle), -np.sin(phase_angle))
    return (waveform * window / math.sqrt(3 * SEG / 8)).astype(np.float32)


def slices_of(value, count):
    parts = []
    for number in range(count):
        part = value.astype(jnp.bfloat16)
        parts.append(part)
        if number + 1 < count:
            value = value - part.astype(jnp.float32)
    return parts


def two_sum(a, b):
    total = a + b
    rest = total - a
    return total, (a - (total - rest)) + (b - rest)


def pair_add(a, b):
    high, low = two_sum(a[0], b[0])
    low = low + (a[1] + b[1])
    total = high + low
    return total, low - (total - high)


def pair_tree(values):
    while len(values) > 1:
        values = [pair_add(values[i], values[i + 1]) for i in range(0, len(values), 2)]
    return values[0]


def halves(a):
    shifted = a * 4097.0
    high = shifted - (shifted - a)
    return high, a - high


def pair_product(a, a_halves, b, b_halves):
    product = a[0] * b[0]
    (ah, al), (bh, bl) = a_halves, b_halves
    error = ((ah * bh - product) + ah * bl + al * bh) + al * bl
    return product, error + (a[0] * b[1] + a[1] * b[0])


def spectrum_body(table_t, records, spec_ref):
    t1, t2, t3 = slices_of(table_t, 3)
    left = jnp.concatenate([t1, t1, t1, t2, t2, t3], axis=1)
    x1, x2, x3 = slices_of(records, 3)
    points = records.shape[1]
    for b in range(NB):
        at = slice(HOP * b, HOP * b + SEG)
        right = jnp.concatenate([x1[at], x2[at], x3[at], x1[at], x2[at], x1[at]], axis=0)
        spec_ref[:, b, :] = jnp.dot(left, right, preferred_element_type=jnp.float32)
    spec_ref[:, NB, :] = jnp.zeros((SEG, points), jnp.float32)


def cut_rows(real, imag):
    top = jnp.maximum(jnp.max(jnp.abs(real), axis=1, keepdims=True), jnp.max(jnp.abs(imag), axis=1, keepdims=True))
    grid = top * (1.5 * 2.0**17)
    cuts = []
    for _ in range(CUTS):
        cut = ((real + grid) - grid, (imag + grid) - grid)
        real, imag = real - cut[0], imag - cut[1]
        grid = grid * 2.0**-7
        cuts.append(cut)
    return cuts


def gram_slot(real, imag, two_real):
    left, right = [], []
    for r, i in cut_rows(real, imag):
        left.append(jnp.concatenate([r, i], axis=1).astype(jnp.bfloat16))
        if two_real is None:
            across, own = i, -r
        else:
            across, own = i * (1.0 - two_real), i * two_real - r * (1.0 - two_real)
        right.append(jnp.concatenate([r, across], axis=1).astype(jnp.bfloat16))
        right.append(jnp.concatenate([across, own], axis=1).astype(jnp.bfloat16))
    products = lax.dot_general(
        jnp.concatenate(left, axis=0),
        jnp.concatenate(right, axis=0),
        (((1,), (1,)), ((), ())),
        preferred_element_type=jnp.float32,
    )

    def block(row, column):
        return products[32 * row:32 * row + 32, 64 * column:64 * column + 64]

    low = None
    for order in reversed(range(2, 2 * CUTS - 1)):
        for row in range(CUTS):
            if 0 <= order - row < CUTS:
                part = block(row, order - row)
                low = part if low is None else low + part
    high, rest = two_sum(block(0, 0), block(0, 1))
    high, more = two_sum(high, block(1, 0))
    low = low + (rest + more)
    total = high + low
    return total, low - (total - high)


def spectrum_kernel(me_ref, table_ref, root_ref, *refs, tm):
    pieces, (spec_ref, keep_ref, send_ref, records_ref) = refs[:tm], refs[tm:]
    rows = pieces[0].shape[0]
    root = root_ref[...]
    for d in range(tm):
        start = pl.multiple_of((me_ref[0] ^ d) * rows, rows)
        records_ref[pl.ds(start, rows), :] = pieces[d][...] * root
    spectrum_body(table_ref[...], records_ref[...], spec_ref)
    core = me_ref[0] & 1
    row = lax.broadcasted_iota(jnp.int32, (32, 32), 0)
    column = lax.broadcasted_iota(jnp.int32, (32, 32), 1)
    for j, out_ref in ((1, send_ref), (0, keep_ref)):
        side = core ^ j
        for q in range(SIDE):
            packed = [[], []]
            for s in range(4):
                slot = (side * SIDE + q) * 4 + s
                special = q == 0 and s == 0
                two_real = jnp.where(side == 0, 1.0, 0.0) if special else None
                sums = gram_slot(spec_ref[slot], spec_ref[SLOTS + slot], two_real)
                for part in range(2):
                    real, imag = sums[part][:, :32], sums[part][:, 32:]
                    square = jnp.where(column >= row, real, imag)
                    diagonal = jnp.sum(jnp.where(column == row, imag, 0.0), axis=0, keepdims=True)
                    if special:
                        square = jnp.where(row == NB, diagonal, square)
                    packed[part].append(square)
            for part in range(2):
                out_ref[q, part] = jnp.concatenate(packed[part], axis=1)


def core_sum_kernel(me_ref, keep_ref, got_ref, *out_refs):
    for d in range(SIDE):
        q = (me_ref[1] & (SIDE - 1)) ^ d
        high, low = pair_add((keep_ref[q, 0], keep_ref[q, 1]), (got_ref[q, 0], got_ref[q, 1]))
        out_refs[d][0] = high
        out_refs[d][1] = low


def pair_sum_kernel(*refs):
    high, low = pair_tree([(ref[0], ref[1]) for ref in refs[:-1]])
    refs[-1][0] = high
    refs[-1][1] = low


def swap_squares(square):
    turned = square.T
    return jnp.concatenate([turned[32 * s:32 * s + 32] for s in range(4)], axis=1)


def factor_kernel(me_ref, *refs, scale):
    out_ref = refs[-1]
    high, low = pair_tree([(ref[0], ref[1]) for ref in refs[:-1]])
    shape = (32, 128)
    row = lax.broadcasted_iota(jnp.int32, shape, 0)
    lane = lax.broadcasted_iota(jnp.int32, shape, 1)
    column = lane % 32
    base = lane - column
    first = jnp.logical_and((me_ref[0] & 1) == 0, (me_ref[1] & (SIDE - 1)) == 0)
    two_real = jnp.logical_and(lane < 32, first)
    sign = jnp.where(two_real, 1.0, -1.0)
    real, imag = [], []
    for square in (high, low):
        turned = swap_squares(square)
        diagonal = jnp.where(two_real, square[NB:NB + 1], 0.0)
        real.append(jnp.where(column >= row, square, turned))
        imag.append(jnp.where(column < row, square, jnp.where(column == row, diagonal, turned * sign)))
    inside = jnp.logical_and(row < NB, column < NB)
    real = [jnp.where(inside, part * scale, 0.0) for part in real]
    imag = [jnp.where(inside, part * scale, 0.0) for part in imag]

    def spread(value, at):
        return jnp.take_along_axis(value, base + at, axis=1, mode="promise_in_bounds")

    def rows_of(value, at):
        return jnp.broadcast_to(value[at:at + 1], shape)

    def quotient(value, pivot, pivot_halves, inverse):
        first_part = value[0] * inverse
        product, error = pair_product(
            (first_part, 0.0), halves(first_part), (pivot[0], 0.0), pivot_halves
        )
        rest = ((value[0] - product) - error) + (value[1] - first_part * pivot[1])
        return first_part, rest * inverse

    def minus(value, products):
        high, low = value[0], value[1]
        for product in products:
            high, error = two_sum(high, -product[0])
            low = low + (error - product[1])
        total = high + low
        return [total, low - (total - high)]

    for k in range(NB):
        line_real = [rows_of(part, k) for part in real]
        line_imag = [rows_of(part, k) for part in imag]
        pivot_real = [spread(part, k) for part in line_real]
        pivot_imag = [jnp.where(two_real, spread(part, k), own) for part, own in zip(line_imag, pivot_real)]
        below = row > k
        here = column == k
        step_real = [jnp.where(below, spread(part, k), 0.0) for part in real]
        step_imag = [jnp.where(below, spread(part, k), 0.0) for part in imag]
        step_real = quotient(step_real, pivot_real, halves(pivot_real[0]), 1.0 / pivot_real[0])
        step_imag = quotient(step_imag, pivot_imag, halves(pivot_imag[0]), 1.0 / pivot_imag[0])
        cross = tuple(jnp.where(two_real, 0.0, part) for part in step_imag)
        own = tuple(jnp.where(two_real, b, a) for a, b in zip(step_real, step_imag))
        one = jnp.where(here, 1.0, 0.0)
        line_real = (jnp.where(here, 1.0, line_real[0]), jnp.where(here, 0.0, line_real[1]))
        line_imag = (
            jnp.where(here, jnp.where(two_real, 1.0, 0.0), line_imag[0]),
            jnp.where(here, 0.0, line_imag[1]),
        )
        clear = jnp.logical_and(below, here)
        real = [jnp.where(clear, 0.0, part) for part in real]
        imag = [jnp.where(clear, 0.0, part) for part in imag]
        line_real_halves, line_imag_halves = halves(line_real[0]), halves(line_imag[0])
        step_halves, cross_halves, own_halves = halves(step_real[0]), halves(cross[0]), halves(own[0])
        p = pair_product(step_real, step_halves, line_real, line_real_halves)
        q = pair_product(cross, cross_halves, line_imag, line_imag_halves)
        real = minus(real, [p, (-q[0], -q[1])])
        p = pair_product(own, own_halves, line_imag, line_imag_halves)
        q = pair_product(cross, cross_halves, line_real, line_real_halves)
        imag = minus(imag, [p, q])
    pivot_real = spread(real[0], row)
    pivot_imag = jnp.where(two_real, spread(imag[0], row), pivot_real)
    good = row < NB
    out_ref[0] = jnp.where(good, real[0] / jnp.sqrt(pivot_real), 0.0)
    out_ref[1] = jnp.where(good, imag[0] / jnp.sqrt(pivot_imag), 0.0)


def apply_kernel(me_ref, *refs):
    pieces, (spec_ref, modes_ref, triangle_ref) = refs[:GROUPS], refs[GROUPS:]
    points = spec_ref.shape[-1]
    tiles = points // 128
    shape = (32, 128)
    row = lax.broadcasted_iota(jnp.int32, shape, 0)
    lane = lax.broadcasted_iota(jnp.int32, shape, 1)
    column = lane % 32
    here = column == row
    zero = jnp.zeros((NB, 128), jnp.float32)

    def put(frequency, part, value):
        for tile in range(tiles):
            modes_ref[frequency, pl.ds(2 * tile + part, NB, stride=2 * tiles), :] = (
                value if value is zero else value[:, 128 * tile:128 * tile + 128]
            )

    put(0, 1, zero)
    put(SLOTS, 1, zero)
    for c in range(2):
        for d in range(SIDE):
            piece = pieces[SIDE * c + d]
            group = ((me_ref[0] & 1) ^ c) * SIDE + ((me_ref[1] & (SIDE - 1)) ^ d)
            is_first = group == 0
            two_real = jnp.logical_and(lane < 32, is_first)
            both_real, both_imag = piece[0], piece[1]
            upper_real = jnp.where(column >= row, both_real, 0.0)
            upper_imag = jnp.where(column >= row, both_imag, 0.0)
            for s in range(4):
                triangle_ref[0, 4 * group + s] = upper_real[:NB, 32 * s:32 * s + NB]
                if s:
                    triangle_ref[1, 4 * group + s] = upper_imag[:NB, 32 * s:32 * s + NB]
                else:
                    triangle_ref[1, 4 * group] = jnp.where(is_first, 0.0, upper_imag[:NB, :NB])
            low_real = jnp.where(column < row, both_real, jnp.where(here, 1.0 / both_real, 0.0))
            low_imag = jnp.where(
                column < row, both_imag, jnp.where(jnp.logical_and(here, two_real), 1.0 / both_imag, 0.0)
            )
            good = row < NB
            low_real = jnp.where(good, low_real, 0.0)
            low_imag = jnp.where(good, low_imag, 0.0)
            cross = jnp.where(two_real, 0.0, low_imag)
            own = jnp.where(two_real, low_imag, low_real)
            rows = []
            for s in range(4):
                mine = lane // 32 == s
                rows.append(jnp.concatenate([jnp.where(mine, low_real, 0.0), jnp.where(mine, cross, 0.0)], axis=1))
                rows.append(jnp.concatenate([jnp.where(mine, -cross, 0.0), jnp.where(mine, own, 0.0)], axis=1))
            left = slices_of(jnp.concatenate(rows, axis=0), 3)
            reals = spec_ref[pl.ds(4 * group, 4)].reshape(128, points)
            imags = spec_ref[pl.ds(SLOTS + 4 * group, 4)].reshape(128, points)
            right = slices_of(jnp.concatenate([reals, imags], axis=0), 3)
            total = None
            for order in reversed(range(3)):
                for number in range(order + 1):
                    part = jnp.dot(left[number], right[order - number], preferred_element_type=jnp.float32)
                    total = part if total is None else total + part
            for s in range(4):
                put(4 * group + s, 0, total[64 * s:64 * s + NB])
                if s:
                    put(4 * group + s, 1, total[64 * s + 32:64 * s + 32 + NB])

            @pl.when(is_first)
            def _(total=total, upper_imag=upper_imag):
                put(SLOTS, 0, total[32:32 + NB])
                triangle_ref[0, SLOTS] = upper_imag[:NB, :NB]
                triangle_ref[1, SLOTS] = jnp.zeros((NB, NB), jnp.float32)

            @pl.when(jnp.logical_not(is_first))
            def _(total=total, group=group):
                put(4 * group, 1, total[32:32 + NB])


def call(body, out_shape, scratch, operands):
    smem = pl.BlockSpec(memory_space=pltpu.SMEM)
    vmem = pl.BlockSpec(memory_space=pltpu.VMEM)
    return pl.pallas_call(
        body,
        out_shape=out_shape,
        in_specs=[smem] + [vmem] * (len(operands) - 1),
        out_specs=jax.tree.map(lambda _: vmem, out_shape),
        scratch_shapes=scratch,
        compiler_params=pltpu.CompilerParams(vmem_limit_bytes=VMEM_BYTES),
    )(*operands)


def f32(*shape):
    return jax.ShapeDtypeStruct(shape, jnp.float32)


def xor_pairs(size, difference):
    return [(i, i ^ difference) for i in range(size)]


def factor_over_devices(place, keep, send, scale):
    tm, pts = lax.axis_size("tm"), lax.axis_size("pts")
    part = f32(2, 32, 128)
    got = lax.ppermute(send, "tm", xor_pairs(tm, 1))
    parts = call(core_sum_kernel, (part,) * SIDE, [], [place, keep, got])
    parts = [parts[0]] + [lax.ppermute(parts[d], "pts", xor_pairs(pts, d)) for d in range(1, SIDE)]
    total = call(lambda _, *refs: pair_sum_kernel(*refs), part, [], [place] + parts)
    if pts > SIDE:
        parts = [total] + [lax.ppermute(total, "pts", xor_pairs(pts, d)) for d in range(SIDE, pts, SIDE)]
        total = call(lambda _, *refs: pair_sum_kernel(*refs), part, [], [place] + parts)
    parts = [total] + [lax.ppermute(total, "tm", xor_pairs(tm, d)) for d in range(2, tm, 2)]
    own = call(functools.partial(factor_kernel, scale=scale), part, [], [place] + parts)
    own = [own] + [lax.ppermute(own, "pts", xor_pairs(pts, d)) for d in range(1, SIDE)]
    return own + [lax.ppermute(piece, "tm", xor_pairs(tm, 1)) for piece in own]


def shards(snapshots, weights):
    tm, pts = lax.axis_size("tm"), lax.axis_size("pts")
    me = lax.axis_index("tm")
    points = weights.shape[0]
    scale = 1.0 / (points * tm * pts)
    pieces = []
    for d in range(tm):
        piece = lax.dynamic_slice_in_dim(snapshots, (me ^ d) * points, points, 1)
        pieces.append(piece if d == 0 else lax.ppermute(piece, "tm", xor_pairs(tm, d)))
    root = jnp.sqrt(weights)[None, :]
    table_t = jnp.asarray(fourier_table().T)
    place = jnp.stack([me, lax.axis_index("pts")]).astype(jnp.int32)
    half = f32(SIDE, 2, 32, 128)
    spec, keep, send = call(
        functools.partial(spectrum_kernel, tm=tm),
        (f32(SEG, 32, points), half, half),
        [pltpu.VMEM((NT, points), jnp.float32)],
        [place, table_t, root] + pieces,
    )
    factors = factor_over_devices(place, keep, send, scale)
    tiles = points // 128
    modes, triangle = call(
        apply_kernel,
        (f32(NF, NB * tiles * 2, 128), f32(2, NF, NB, NB)),
        [],
        [place] + factors + [spec],
    )
    modes = modes.reshape(NF, NB, tiles, 2, 128).transpose(3, 0, 1, 2, 4).reshape(2, NF, NB, points)
    return (modes, triangle)


def solution(mesh):
    placed = (P("tm", "pts"), P(("pts", "tm")))
    return jax.shard_map(
        shards,
        mesh=mesh,
        in_specs=placed,
        out_specs=(P(None, None, None, ("pts", "tm")), P()),
        check_vma=False,
    )
```

```python
import functools
import math

import jax
import jax.numpy as jnp
import numpy as np
from jax import lax
from jax.experimental import pallas as pl
from jax.experimental.pallas import tpu as pltpu
from jax.sharding import PartitionSpec as P

SEG = 64
HOP = 32
NF = 33
NT = 1024
NB = 31
SLOTS = 32
GROUPS = 8
SIDE = 4
CUTS = 4
VMEM_BYTES = 24 * 1024 * 1024


def fourier_table():
    sample = np.arange(SEG, dtype=np.float64)[:, None]
    column = np.arange(SEG)[None, :]
    frequency = np.where(column < NF, column, column - HOP).astype(np.float64)
    window = 0.5 - 0.5 * np.cos(2.0 * math.pi * sample / SEG)
    phase_angle = 2.0 * math.pi * frequency * sample / SEG
    waveform = np.where(column < NF, np.cos(phase_angle), -np.sin(phase_angle))
    return (waveform * window / math.sqrt(3 * SEG / 8)).astype(np.float32)


def slices_of(value, count):
    parts = []
    for number in range(count):
        part = value.astype(jnp.bfloat16)
        parts.append(part)
        if number + 1 < count:
            value = value - part.astype(jnp.float32)
    return parts


def two_sum(a, b):
    total = a + b
    rest = total - a
    return total, (a - (total - rest)) + (b - rest)


def pair_add(a, b):
    high, low = two_sum(a[0], b[0])
    low = low + (a[1] + b[1])
    total = high + low
    return total, low - (total - high)


def pair_tree(values):
    while len(values) > 1:
        values = [pair_add(values[i], values[i + 1]) for i in range(0, len(values), 2)]
    return values[0]


def halves(a):
    shifted = a * 4097.0
    high = shifted - (shifted - a)
    return high, a - high


def pair_product(a, a_halves, b, b_halves):
    product = a[0] * b[0]
    (ah, al), (bh, bl) = a_halves, b_halves
    error = ((ah * bh - product) + ah * bl + al * bh) + al * bl
    return product, error + (a[0] * b[1] + a[1] * b[0])


def spectrum_body(table_t, records, spec_ref):
    t1, t2, t3 = slices_of(table_t, 3)
    left = jnp.concatenate([t1, t1, t1, t2, t2, t3], axis=1)
    x1, x2, x3 = slices_of(records, 3)
    points = records.shape[1]
    for b in range(NB):
        at = slice(HOP * b, HOP * b + SEG)
        right = jnp.concatenate([x1[at], x2[at], x3[at], x1[at], x2[at], x1[at]], axis=0)
        spec_ref[:, b, :] = jnp.dot(left, right, preferred_element_type=jnp.float32)
    spec_ref[:, NB, :] = jnp.zeros((SEG, points), jnp.float32)


def cut_rows(real, imag):
    top = jnp.maximum(jnp.max(jnp.abs(real), axis=1, keepdims=True), jnp.max(jnp.abs(imag), axis=1, keepdims=True))
    grid = top * (1.5 * 2.0**17)
    cuts = []
    for _ in range(CUTS):
        cut = ((real + grid) - grid, (imag + grid) - grid)
        real, imag = real - cut[0], imag - cut[1]
        grid = grid * 2.0**-7
        cuts.append(cut)
    return cuts


def gram_slot(real, imag, two_real):
    rows = jnp.concatenate([part for cut in cut_rows(real, imag) for part in cut], axis=0).astype(jnp.bfloat16)
    products = lax.dot_general(rows, rows, (((1,), (1,)), ((), ())), preferred_element_type=jnp.float32)
    lane = lax.broadcasted_iota(jnp.int32, (32, 128), 1)
    is_real = lane // 32 % 2 == 0
    front = lane < 64

    def block(number, half):
        return products[32 * number:32 * number + 32, 128 * half:128 * half + 128]

    def combine(from_real, from_imag):
        swapped = jnp.take_along_axis(from_imag, lane ^ 32, axis=1, mode="promise_in_bounds")
        result = from_real + jnp.where(is_real, swapped, -swapped)
        if two_real is None:
            return result
        return jnp.where(two_real, jnp.where(is_real, from_real, from_imag), result)

    first = combine(block(0, 0), block(1, 0))
    second = combine(block(2, 0), block(3, 0))
    rest_real, rest_imag = (
        block(6 + part, 1) + (block(4 + part, 1) + block(6 + part, 0)) + (block(2 + part, 1) + block(4 + part, 0)) + block(part, 1)
        for part in range(2)
    )
    low = combine(rest_real, rest_imag) + jnp.where(front, 0.0, second)
    low = low[:, :64] + low[:, 64:]
    high, rest = two_sum(first[:, :64], first[:, 64:])
    high, more = two_sum(high, second[:, :64])
    low = low + (rest + more)
    total = high + low
    return total, low - (total - high)


def spectrum_kernel(me_ref, table_ref, root_ref, *refs, tm):
    pieces, (spec_ref, keep_ref, send_ref, records_ref) = refs[:tm], refs[tm:]
    rows = pieces[0].shape[0]
    root = root_ref[...]
    for d in range(tm):
        start = pl.multiple_of((me_ref[0] ^ d) * rows, rows)
        records_ref[pl.ds(start, rows), :] = pieces[d][...] * root
    spectrum_body(table_ref[...], records_ref[...], spec_ref)
    core = me_ref[0] & 1
    row = lax.broadcasted_iota(jnp.int32, (32, 32), 0)
    column = lax.broadcasted_iota(jnp.int32, (32, 32), 1)
    for j, out_ref in ((1, send_ref), (0, keep_ref)):
        side = core ^ j
        for q in range(SIDE):
            packed = [[], []]
            for s in range(4):
                slot = (side * SIDE + q) * 4 + s
                special = q == 0 and s == 0
                two_real = side == 0 if special else None
                sums = gram_slot(spec_ref[slot], spec_ref[SLOTS + slot], two_real)
                for part in range(2):
                    real, imag = sums[part][:, :32], sums[part][:, 32:]
                    square = jnp.where(column >= row, real, imag)
                    if special:
                        diagonal = jnp.sum(jnp.where(column == row, imag, 0.0), axis=0, keepdims=True)
                        square = jnp.where(row == NB, diagonal, square)
                    packed[part].append(square)
            for part in range(2):
                out_ref[q, part] = jnp.concatenate(packed[part], axis=1)


def core_sum_kernel(me_ref, keep_ref, got_ref, *out_refs):
    for d in range(SIDE):
        q = (me_ref[1] & (SIDE - 1)) ^ d
        high, low = pair_add((keep_ref[q, 0], keep_ref[q, 1]), (got_ref[q, 0], got_ref[q, 1]))
        out_refs[d][0] = high
        out_refs[d][1] = low


def pair_sum_kernel(*refs):
    high, low = pair_tree([(ref[0], ref[1]) for ref in refs[:-1]])
    refs[-1][0] = high
    refs[-1][1] = low


def swap_squares(square):
    turned = square.T
    return jnp.concatenate([turned[32 * s:32 * s + 32] for s in range(4)], axis=1)


def factor_kernel(me_ref, *refs, scale):
    out_ref = refs[-1]
    high, low = pair_tree([(ref[0], ref[1]) for ref in refs[:-1]])
    shape = (32, 128)
    row = lax.broadcasted_iota(jnp.int32, shape, 0)
    lane = lax.broadcasted_iota(jnp.int32, shape, 1)
    column = lane % 32
    base = lane - column
    first = jnp.logical_and((me_ref[0] & 1) == 0, (me_ref[1] & (SIDE - 1)) == 0)
    two_real = jnp.logical_and(lane < 32, first)
    sign = jnp.where(two_real, 1.0, -1.0)
    real, imag = [], []
    for square in (high, low):
        turned = swap_squares(square)
        diagonal = jnp.where(two_real, square[NB:NB + 1], 0.0)
        real.append(jnp.where(column >= row, square, turned))
        imag.append(jnp.where(column < row, square, jnp.where(column == row, diagonal, turned * sign)))
    inside = jnp.logical_and(row < NB, column < NB)
    real = [jnp.where(inside, part * scale, 0.0) for part in real]
    imag = [jnp.where(inside, part * scale, 0.0) for part in imag]

    def spread(value, at):
        return jnp.take_along_axis(value, base + at, axis=1, mode="promise_in_bounds")

    def rows_of(value, at):
        return jnp.broadcast_to(value[at:at + 1], shape)

    def quotient(value, pivot, pivot_halves, inverse):
        first_part = value[0] * inverse
        product, error = pair_product(
            (first_part, 0.0), halves(first_part), (pivot[0], 0.0), pivot_halves
        )
        rest = ((value[0] - product) - error) + (value[1] - first_part * pivot[1])
        return first_part, rest * inverse

    def minus(value, products):
        high, low = value[0], value[1]
        for product in products:
            high, error = two_sum(high, -product[0])
            low = low + (error - product[1])
        total = high + low
        return [total, low - (total - high)]

    for k in range(NB):
        line_real = [rows_of(part, k) for part in real]
        line_imag = [rows_of(part, k) for part in imag]
        pivot_real = [spread(part, k) for part in line_real]
        pivot_imag = [jnp.where(two_real, spread(part, k), own) for part, own in zip(line_imag, pivot_real)]
        below = row > k
        here = column == k
        step_real = [jnp.where(below, spread(part, k), 0.0) for part in real]
        step_imag = [jnp.where(below, spread(part, k), 0.0) for part in imag]
        step_real = quotient(step_real, pivot_real, halves(pivot_real[0]), 1.0 / pivot_real[0])
        step_imag = quotient(step_imag, pivot_imag, halves(pivot_imag[0]), 1.0 / pivot_imag[0])
        cross = tuple(jnp.where(two_real, 0.0, part) for part in step_imag)
        own = tuple(jnp.where(two_real, b, a) for a, b in zip(step_real, step_imag))
        one = jnp.where(here, 1.0, 0.0)
        line_real = (jnp.where(here, 1.0, line_real[0]), jnp.where(here, 0.0, line_real[1]))
        line_imag = (
            jnp.where(here, jnp.where(two_real, 1.0, 0.0), line_imag[0]),
            jnp.where(here, 0.0, line_imag[1]),
        )
        clear = jnp.logical_and(below, here)
        real = [jnp.where(clear, 0.0, part) for part in real]
        imag = [jnp.where(clear, 0.0, part) for part in imag]
        line_real_halves, line_imag_halves = halves(line_real[0]), halves(line_imag[0])
        step_halves, cross_halves, own_halves = halves(step_real[0]), halves(cross[0]), halves(own[0])
        p = pair_product(step_real, step_halves, line_real, line_real_halves)
        q = pair_product(cross, cross_halves, line_imag, line_imag_halves)
        real = minus(real, [p, (-q[0], -q[1])])
        p = pair_product(own, own_halves, line_imag, line_imag_halves)
        q = pair_product(cross, cross_halves, line_real, line_real_halves)
        imag = minus(imag, [p, q])
    pivot_real = spread(real[0], row)
    pivot_imag = jnp.where(two_real, spread(imag[0], row), pivot_real)
    good = row < NB
    out_ref[0] = jnp.where(good, real[0] / jnp.sqrt(pivot_real), 0.0)
    out_ref[1] = jnp.where(good, imag[0] / jnp.sqrt(pivot_imag), 0.0)


def apply_kernel(me_ref, *refs):
    pieces, (spec_ref, modes_ref, triangle_ref, tiles_ref, sent) = refs[:GROUPS], refs[GROUPS:]
    points = spec_ref.shape[-1]
    shape = (32, 128)
    row = lax.broadcasted_iota(jnp.int32, shape, 0)
    lane = lax.broadcasted_iota(jnp.int32, shape, 1)
    column = lane % 32
    here = column == row
    even = lane // 32 % 2 == 0
    wide = lax.broadcasted_iota(jnp.int32, (64, 128), 1) < 64
    nothing = jnp.zeros((32, 128), jnp.float32)
    copies = []

    def put(frequency, real, imag):
        rows = []
        for tile in range(points // 128):
            at = slice(128 * tile, 128 * tile + 128)
            rows += [real[:, at], nothing if imag is None else imag[:, at]]
        number = len(copies)
        tiles_ref[number] = jnp.swapaxes(jnp.stack(rows, axis=0), 0, 1)[:NB]
        copy = pltpu.make_async_copy(tiles_ref.at[number], modes_ref.at[frequency], sent.at[number])
        copy.start()
        copies.append(copy)

    last_real = jnp.zeros((32, points), jnp.float32)
    last_triangle = jnp.zeros((NB, NB), jnp.float32)
    for c in range(2):
        for d in range(SIDE):
            piece = pieces[SIDE * c + d]
            group = ((me_ref[0] & 1) ^ c) * SIDE + ((me_ref[1] & (SIDE - 1)) ^ d)
            is_first = group == 0
            both_real, both_imag = piece[0], piece[1]
            upper_real = jnp.where(column >= row, both_real, 0.0)
            upper_imag = jnp.where(column >= row, both_imag, 0.0)
            two_real = jnp.logical_and(lane < 32, is_first)
            low_real = jnp.where(column < row, both_real, jnp.where(here, 1.0 / both_real, 0.0))
            low_imag = jnp.where(
                column < row, both_imag, jnp.where(jnp.logical_and(here, two_real), 1.0 / both_imag, 0.0)
            )
            good = row < NB
            low_real = jnp.where(good, low_real, 0.0)
            low_imag = jnp.where(good, low_imag, 0.0)
            cross = jnp.where(two_real, 0.0, low_imag)
            own = jnp.where(two_real, low_imag, low_real)
            for s in range(4):
                slot = 4 * group + s

                def spread(value):
                    return jnp.take_along_axis(value, 32 * s + column, axis=1, mode="promise_in_bounds")

                wide_cross = spread(cross)
                top = jnp.where(even, spread(low_real), wide_cross)
                bottom = jnp.where(even, -wide_cross, spread(own))
                l0, l1, l2 = (part.astype(jnp.float32) for part in slices_of(jnp.concatenate([top, bottom], axis=0), 3))
                left = [l0, jnp.where(wide, l1, l0), jnp.where(wide, l1, l2)]
                left = jnp.concatenate([part.astype(jnp.bfloat16) for part in left], axis=1)
                r0, r1, r2 = slices_of(jnp.concatenate([spec_ref[slot], spec_ref[SLOTS + slot]], axis=0), 3)
                right = jnp.concatenate([r0, r1, r0, r2, r1, r0], axis=0)
                out = jnp.dot(left, right, preferred_element_type=jnp.float32)
                real, imag = out[:32], out[32:]
                square = upper_imag[:NB, 32 * s:32 * s + NB]
                if s == 0:
                    last_real = jnp.where(is_first, imag, last_real)
                    last_triangle = jnp.where(is_first, square, last_triangle)
                    imag = jnp.where(is_first, 0.0, imag)
                    square = jnp.where(is_first, 0.0, square)
                put(slot, real, imag)
                triangle_ref[0, slot] = upper_real[:NB, 32 * s:32 * s + NB]
                triangle_ref[1, slot] = square
    put(SLOTS, last_real, None)
    triangle_ref[0, SLOTS] = last_triangle
    triangle_ref[1, SLOTS] = jnp.zeros((NB, NB), jnp.float32)
    for copy in copies:
        copy.wait()


def call(body, out_shape, scratch, operands, out_spaces=None):
    smem = pl.BlockSpec(memory_space=pltpu.SMEM)
    vmem = pl.BlockSpec(memory_space=pltpu.VMEM)
    return pl.pallas_call(
        body,
        out_shape=out_shape,
        in_specs=[smem] + [vmem] * (len(operands) - 1),
        out_specs=[pl.BlockSpec(memory_space=space) for space in out_spaces] if out_spaces else jax.tree.map(lambda _: vmem, out_shape),
        scratch_shapes=scratch,
        compiler_params=pltpu.CompilerParams(vmem_limit_bytes=VMEM_BYTES),
    )(*operands)


def f32(*shape):
    return jax.ShapeDtypeStruct(shape, jnp.float32)


def xor_pairs(size, difference):
    return [(i, i ^ difference) for i in range(size)]


def factor_over_devices(place, keep, send, scale):
    tm, pts = lax.axis_size("tm"), lax.axis_size("pts")
    part = f32(2, 32, 128)
    got = lax.ppermute(send, "tm", xor_pairs(tm, 1))
    parts = call(core_sum_kernel, (part,) * SIDE, [], [place, keep, got])
    parts = [parts[0]] + [lax.ppermute(parts[d], "pts", xor_pairs(pts, d)) for d in range(1, SIDE)]
    total = call(lambda _, *refs: pair_sum_kernel(*refs), part, [], [place] + parts)
    if pts > SIDE:
        parts = [total] + [lax.ppermute(total, "pts", xor_pairs(pts, d)) for d in range(SIDE, pts, SIDE)]
        total = call(lambda _, *refs: pair_sum_kernel(*refs), part, [], [place] + parts)
    parts = [total] + [lax.ppermute(total, "tm", xor_pairs(tm, d)) for d in range(2, tm, 2)]
    own = call(functools.partial(factor_kernel, scale=scale), part, [], [place] + parts)
    own = [own] + [lax.ppermute(own, "pts", xor_pairs(pts, d)) for d in range(1, SIDE)]
    return own + [lax.ppermute(piece, "tm", xor_pairs(tm, 1)) for piece in own]


def shards(snapshots, weights):
    tm, pts = lax.axis_size("tm"), lax.axis_size("pts")
    me = lax.axis_index("tm")
    points = weights.shape[0]
    scale = 1.0 / (points * tm * pts)
    pieces = []
    for d in range(tm):
        piece = lax.dynamic_slice_in_dim(snapshots, (me ^ d) * points, points, 1)
        pieces.append(piece if d == 0 else lax.ppermute(piece, "tm", xor_pairs(tm, d)))
    root = jnp.sqrt(weights)[None, :]
    table_t = jnp.asarray(fourier_table().T)
    place = jnp.stack([me, lax.axis_index("pts")]).astype(jnp.int32)
    half = f32(SIDE, 2, 32, 128)
    spec, keep, send = call(
        functools.partial(spectrum_kernel, tm=tm),
        (f32(SEG, 32, points), half, half),
        [pltpu.VMEM((NT, points), jnp.float32)],
        [place, table_t, root] + pieces,
    )
    factors = factor_over_devices(place, keep, send, scale)
    tiles = points // 128
    modes, triangle = call(
        apply_kernel,
        (f32(NF, NB, tiles * 2, 128), f32(2, NF, NB, NB)),
        [pltpu.VMEM((NF, NB, tiles * 2, 128), jnp.float32), pltpu.SemaphoreType.DMA((NF,))],
        [place] + factors + [spec],
        [pl.ANY, pltpu.VMEM],
    )
    modes = modes.reshape(NF, NB, tiles, 2, 128).transpose(3, 0, 1, 2, 4).reshape(2, NF, NB, points)
    return (modes, triangle)


def solution(mesh):
    placed = (P("tm", "pts"), P(("pts", "tm")))
    return jax.shard_map(
        shards,
        mesh=mesh,
        in_specs=placed,
        out_specs=(P(None, None, None, ("pts", "tm")), P()),
        check_vma=False,
    )
```

```python
import functools
import math

import jax
import jax.numpy as jnp
import numpy as np
from jax import lax
from jax.experimental import pallas as pl
from jax.experimental.pallas import tpu as pltpu
from jax.sharding import PartitionSpec as P

SEG = 64
HOP = 32
NF = 33
NT = 1024
NB = 31
SLOTS = 32
GROUPS = 8
SIDE = 4
CUTS = 4
VMEM_BYTES = 24 * 1024 * 1024


def fourier_table():
    sample = np.arange(SEG, dtype=np.float64)[:, None]
    column = np.arange(SEG)[None, :]
    frequency = np.where(column < NF, column, column - HOP).astype(np.float64)
    window = 0.5 - 0.5 * np.cos(2.0 * math.pi * sample / SEG)
    phase_angle = 2.0 * math.pi * frequency * sample / SEG
    waveform = np.where(column < NF, np.cos(phase_angle), -np.sin(phase_angle))
    return (waveform * window / math.sqrt(3 * SEG / 8)).astype(np.float32)


def slices_of(value, count):
    parts = []
    for number in range(count):
        part = value.astype(jnp.bfloat16)
        parts.append(part)
        if number + 1 < count:
            value = value - part.astype(jnp.float32)
    return parts


def two_sum(a, b):
    total = a + b
    rest = total - a
    return total, (a - (total - rest)) + (b - rest)


def pair_add(a, b):
    high, low = two_sum(a[0], b[0])
    low = low + (a[1] + b[1])
    total = high + low
    return total, low - (total - high)


def pair_tree(values):
    while len(values) > 1:
        values = [pair_add(values[i], values[i + 1]) for i in range(0, len(values), 2)]
    return values[0]


def halves(a):
    shifted = a * 4097.0
    high = shifted - (shifted - a)
    return high, a - high


def pair_product(a, a_halves, b, b_halves):
    product = a[0] * b[0]
    (ah, al), (bh, bl) = a_halves, b_halves
    error = ((ah * bh - product) + ah * bl + al * bh) + al * bl
    return product, error + (a[0] * b[1] + a[1] * b[0])


def spectrum_body(table_t, records, spec_ref):
    halves_t = jnp.concatenate([table_t[:, :HOP], table_t[:, HOP:]], axis=0)
    t1, t2, t3 = slices_of(halves_t, 3)
    left = jnp.concatenate([t1, t1, t1, t2, t2, t3], axis=1)
    x1, x2, x3 = slices_of(records, 3)
    before = None
    for hop in range(NT // HOP):
        at = slice(HOP * hop, HOP * hop + HOP)
        right = jnp.concatenate([x1[at], x2[at], x3[at], x1[at], x2[at], x1[at]], axis=0)
        out = jnp.dot(left, right, preferred_element_type=jnp.float32)
        if hop:
            spec_ref[:, hop - 1, :] = before + out[SEG:]
        before = out[:SEG]
    spec_ref[:, NB, :] = jnp.zeros((SEG, records.shape[1]), jnp.float32)


def cut_rows(real, imag):
    top = jnp.maximum(jnp.max(jnp.abs(real), axis=1, keepdims=True), jnp.max(jnp.abs(imag), axis=1, keepdims=True))
    grid = top * (1.5 * 2.0**17)
    cuts = []
    for _ in range(CUTS):
        cut = ((real + grid) - grid, (imag + grid) - grid)
        real, imag = real - cut[0], imag - cut[1]
        grid = grid * 2.0**-7
        cuts.append(cut)
    return cuts


def gram_products(real, imag):
    rows = jnp.concatenate([part for cut in cut_rows(real, imag) for part in cut], axis=0).astype(jnp.bfloat16)
    return lax.dot_general(rows, rows, (((1,), (1,)), ((), ())), preferred_element_type=jnp.float32)


def gram_pairs(products, two_real):
    lane = lax.broadcasted_iota(jnp.int32, (32, 128), 1)
    is_real = lane // 32 % 2 == 0
    front = lane < 64

    def block(number, half):
        return products[32 * number:32 * number + 32, 128 * half:128 * half + 128]

    def combine(from_real, from_imag):
        swapped = jnp.take_along_axis(from_imag, lane ^ 32, axis=1, mode="promise_in_bounds")
        result = from_real + jnp.where(is_real, swapped, -swapped)
        if two_real is None:
            return result
        return jnp.where(two_real, jnp.where(is_real, from_real, from_imag), result)

    first = combine(block(0, 0), block(1, 0))
    second = combine(block(2, 0), block(3, 0))
    rest_real, rest_imag = (
        block(6 + part, 1) + (block(4 + part, 1) + block(6 + part, 0)) + (block(2 + part, 1) + block(4 + part, 0)) + block(part, 1)
        for part in range(2)
    )
    low = combine(rest_real, rest_imag) + jnp.where(front, 0.0, second)
    low = low[:, :64] + low[:, 64:]
    high, rest = two_sum(first[:, :64], first[:, 64:])
    high, more = two_sum(high, second[:, :64])
    low = low + (rest + more)
    total = high + low
    return total, low - (total - high)


def spectrum_kernel(me_ref, table_ref, root_ref, *refs, places):
    pieces, (spec_ref, keep_ref, send_ref, records_ref) = refs[:len(places)], refs[len(places):]
    for (d, first), piece in zip(places, pieces):
        rows, size = piece.shape
        start = pl.multiple_of((me_ref[0] ^ d) * rows, rows)
        at = slice(first, first + size)
        records_ref[pl.ds(start, rows), at] = piece[...] * root_ref[:, at]
    spectrum_body(table_ref[...], records_ref[...], spec_ref)
    core = me_ref[0] & 1
    row = lax.broadcasted_iota(jnp.int32, (32, 32), 0)
    column = lax.broadcasted_iota(jnp.int32, (32, 32), 1)
    order = [(j, q, s) for j in (1, 0) for q in range(SIDE) for s in range(4)]

    def products_of(step):
        j, q, s = order[step]
        slot = ((core ^ j) * SIDE + q) * 4 + s
        return gram_products(spec_ref[slot], spec_ref[SLOTS + slot])

    ahead = products_of(0)
    for step, (j, q, s) in enumerate(order):
        products = ahead
        if step + 1 < len(order):
            ahead = products_of(step + 1)
        special = q == 0 and s == 0
        if s == 0:
            packed = [[], []]
        sums = gram_pairs(products, (core ^ j) == 0 if special else None)
        for part in range(2):
            real, imag = sums[part][:, :32], sums[part][:, 32:]
            square = jnp.where(column >= row, real, imag)
            if special:
                diagonal = jnp.sum(jnp.where(column == row, imag, 0.0), axis=0, keepdims=True)
                square = jnp.where(row == NB, diagonal, square)
            packed[part].append(square)
            if s == 3:
                (keep_ref, send_ref)[j][q, part] = jnp.concatenate(packed[part], axis=1)


def core_sum_kernel(me_ref, keep_ref, got_ref, *out_refs):
    for d in range(SIDE):
        q = (me_ref[1] & (SIDE - 1)) ^ d
        high, low = pair_add((keep_ref[q, 0], keep_ref[q, 1]), (got_ref[q, 0], got_ref[q, 1]))
        out_refs[d][0] = high
        out_refs[d][1] = low


def pair_sum_kernel(*refs):
    high, low = pair_tree([(ref[0], ref[1]) for ref in refs[:-1]])
    refs[-1][0] = high
    refs[-1][1] = low


def swap_squares(square):
    turned = square.T
    return jnp.concatenate([turned[32 * s:32 * s + 32] for s in range(4)], axis=1)


def factor_kernel(me_ref, *refs, scale):
    out_ref = refs[-1]
    high, low = pair_tree([(ref[0], ref[1]) for ref in refs[:-1]])
    shape = (32, 128)
    row = lax.broadcasted_iota(jnp.int32, shape, 0)
    lane = lax.broadcasted_iota(jnp.int32, shape, 1)
    column = lane % 32
    first = jnp.logical_and((me_ref[0] & 1) == 0, (me_ref[1] & (SIDE - 1)) == 0)
    two_real = jnp.logical_and(lane < 32, first)
    sign = jnp.where(two_real, 1.0, -1.0)
    real, imag = [], []
    for square in (high, low):
        turned = swap_squares(square)
        diagonal = jnp.where(two_real, square[NB:NB + 1], 0.0)
        real.append(jnp.where(column >= row, square, turned))
        imag.append(jnp.where(column < row, square, jnp.where(column == row, diagonal, turned * sign)))
    inside = jnp.logical_and(row < NB, column < NB)
    real = [jnp.where(inside, part * scale, 0.0) for part in real]
    imag = [jnp.where(inside, part * scale, 0.0) for part in imag]

    shape = (8, 128)
    row = lax.broadcasted_iota(jnp.int32, shape, 0)
    lane = lax.broadcasted_iota(jnp.int32, shape, 1)
    column = lane % 32
    base = lane - column
    two_real = jnp.logical_and(lane < 32, first)
    real = [[part[8 * i:8 * i + 8] for part in real] for i in range(4)]
    imag = [[part[8 * i:8 * i + 8] for part in imag] for i in range(4)]

    def spread(value, at):
        return jnp.take_along_axis(value, base + at, axis=1, mode="promise_in_bounds")

    def quotient(value, pivot, pivot_halves, inverse):
        first_part = value[0] * inverse
        product, error = pair_product((first_part, 0.0), halves(first_part), (pivot[0], 0.0), pivot_halves)
        rest = ((value[0] - product) - error) + (value[1] - first_part * pivot[1])
        return first_part, rest * inverse

    def minus(value, products):
        high, low = value[0], value[1]
        for product in products:
            high, error = two_sum(high, -product[0])
            low = low + (error - product[1])
        total = high + low
        return [total, low - (total - high)]

    for k in range(NB):
        at = k % 8
        line_real = [jnp.broadcast_to(part[at:at + 1], shape) for part in real[k // 8]]
        line_imag = [jnp.broadcast_to(part[at:at + 1], shape) for part in imag[k // 8]]
        pivot_real = [spread(part, k) for part in line_real]
        pivot_imag = [jnp.where(two_real, spread(part, k), own) for part, own in zip(line_imag, pivot_real)]
        real_halves, imag_halves = halves(pivot_real[0]), halves(pivot_imag[0])
        real_inverse = 1.0 / pivot_real[0]
        imag_inverse = jnp.where(two_real, 1.0 / pivot_imag[0], real_inverse)
        here = column == k
        line_real = (jnp.where(here, 1.0, line_real[0]), jnp.where(here, 0.0, line_real[1]))
        line_imag = (
            jnp.where(here, jnp.where(two_real, 1.0, 0.0), line_imag[0]),
            jnp.where(here, 0.0, line_imag[1]),
        )
        line_real_halves, line_imag_halves = halves(line_real[0]), halves(line_imag[0])
        for i in range((k + 1) // 8, 4):
            some = 8 * i <= k
            below = row > k - 8 * i
            step_real = [spread(part, k) for part in real[i]]
            step_imag = [spread(part, k) for part in imag[i]]
            if some:
                step_real = [jnp.where(below, part, 0.0) for part in step_real]
                step_imag = [jnp.where(below, part, 0.0) for part in step_imag]
            step_real = quotient(step_real, pivot_real, real_halves, real_inverse)
            step_imag = quotient(step_imag, pivot_imag, imag_halves, imag_inverse)
            cross = tuple(jnp.where(two_real, 0.0, part) for part in step_imag)
            own = tuple(jnp.where(two_real, b, a) for a, b in zip(step_real, step_imag))
            clear = jnp.logical_and(below, here) if some else here
            block_real = [jnp.where(clear, 0.0, part) for part in real[i]]
            block_imag = [jnp.where(clear, 0.0, part) for part in imag[i]]
            step_halves, cross_halves, own_halves = halves(step_real[0]), halves(cross[0]), halves(own[0])
            p = pair_product(step_real, step_halves, line_real, line_real_halves)
            q = pair_product(cross, cross_halves, line_imag, line_imag_halves)
            real[i] = minus(block_real, [p, (-q[0], -q[1])])
            p = pair_product(own, own_halves, line_imag, line_imag_halves)
            q = pair_product(cross, cross_halves, line_real, line_real_halves)
            imag[i] = minus(block_imag, [p, q])
    for i in range(4):
        at = slice(8 * i, 8 * i + 8)
        pivot_real = spread(real[i][0], row + 8 * i)
        pivot_imag = jnp.where(two_real, spread(imag[i][0], row + 8 * i), pivot_real)
        good = row + 8 * i < NB
        out_ref[0, at] = jnp.where(good, real[i][0] / jnp.sqrt(pivot_real), 0.0)
        out_ref[1, at] = jnp.where(good, imag[i][0] / jnp.sqrt(pivot_imag), 0.0)


def apply_kernel(me_ref, *refs):
    pieces, (spec_ref, modes_ref, triangle_ref, tiles_ref, sent) = refs[:GROUPS], refs[GROUPS:]
    points = spec_ref.shape[-1]
    shape = (32, 128)
    row = lax.broadcasted_iota(jnp.int32, shape, 0)
    lane = lax.broadcasted_iota(jnp.int32, shape, 1)
    column = lane % 32
    here = column == row
    even = lane // 32 % 2 == 0
    wide = lax.broadcasted_iota(jnp.int32, (64, 128), 1) < 64
    nothing = jnp.zeros((32, 128), jnp.float32)
    copies = []

    def put(frequency, real, imag):
        rows = []
        for tile in range(points // 128):
            at = slice(128 * tile, 128 * tile + 128)
            rows += [real[:, at], nothing if imag is None else imag[:, at]]
        number = len(copies)
        tiles_ref[number] = jnp.swapaxes(jnp.stack(rows, axis=0), 0, 1)[:NB]
        copy = pltpu.make_async_copy(tiles_ref.at[number], modes_ref.at[frequency], sent.at[number])
        copy.start()
        copies.append(copy)

    last_real = jnp.zeros((32, points), jnp.float32)
    last_triangle = jnp.zeros((NB, NB), jnp.float32)
    for c in range(2):
        for d in range(SIDE):
            piece = pieces[SIDE * c + d]
            group = ((me_ref[0] & 1) ^ c) * SIDE + ((me_ref[1] & (SIDE - 1)) ^ d)
            is_first = group == 0
            both_real, both_imag = piece[0], piece[1]
            upper_real = jnp.where(column >= row, both_real, 0.0)
            upper_imag = jnp.where(column >= row, both_imag, 0.0)
            two_real = jnp.logical_and(lane < 32, is_first)
            low_real = jnp.where(column < row, both_real, jnp.where(here, 1.0 / both_real, 0.0))
            low_imag = jnp.where(
                column < row, both_imag, jnp.where(jnp.logical_and(here, two_real), 1.0 / both_imag, 0.0)
            )
            good = row < NB
            low_real = jnp.where(good, low_real, 0.0)
            low_imag = jnp.where(good, low_imag, 0.0)
            cross = jnp.where(two_real, 0.0, low_imag)
            own = jnp.where(two_real, low_imag, low_real)
            for s in range(4):
                slot = 4 * group + s

                def spread(value):
                    return jnp.take_along_axis(value, 32 * s + column, axis=1, mode="promise_in_bounds")

                wide_cross = spread(cross)
                top = jnp.where(even, spread(low_real), wide_cross)
                bottom = jnp.where(even, -wide_cross, spread(own))
                l0, l1, l2 = (part.astype(jnp.float32) for part in slices_of(jnp.concatenate([top, bottom], axis=0), 3))
                left = [l0, jnp.where(wide, l1, l0), jnp.where(wide, l1, l2)]
                left = jnp.concatenate([part.astype(jnp.bfloat16) for part in left], axis=1)
                r0, r1, r2 = slices_of(jnp.concatenate([spec_ref[slot], spec_ref[SLOTS + slot]], axis=0), 3)
                right = jnp.concatenate([r0, r1, r0, r2, r1, r0], axis=0)
                out = jnp.dot(left, right, preferred_element_type=jnp.float32)
                real, imag = out[:32], out[32:]
                square = upper_imag[:NB, 32 * s:32 * s + NB]
                if s == 0:
                    last_real = jnp.where(is_first, imag, last_real)
                    last_triangle = jnp.where(is_first, square, last_triangle)
                    imag = jnp.where(is_first, 0.0, imag)
                    square = jnp.where(is_first, 0.0, square)
                put(slot, real, imag)
                triangle_ref[0, slot] = upper_real[:NB, 32 * s:32 * s + NB]
                triangle_ref[1, slot] = square
    put(SLOTS, last_real, None)
    triangle_ref[0, SLOTS] = last_triangle
    triangle_ref[1, SLOTS] = jnp.zeros((NB, NB), jnp.float32)
    for copy in copies:
        copy.wait()


def call(body, out_shape, scratch, operands, out_spaces=None):
    smem = pl.BlockSpec(memory_space=pltpu.SMEM)
    vmem = pl.BlockSpec(memory_space=pltpu.VMEM)
    return pl.pallas_call(
        body,
        out_shape=out_shape,
        in_specs=[smem] + [vmem] * (len(operands) - 1),
        out_specs=[pl.BlockSpec(memory_space=space) for space in out_spaces] if out_spaces else jax.tree.map(lambda _: vmem, out_shape),
        scratch_shapes=scratch,
        compiler_params=pltpu.CompilerParams(vmem_limit_bytes=VMEM_BYTES),
    )(*operands)


def f32(*shape):
    return jax.ShapeDtypeStruct(shape, jnp.float32)


def xor_pairs(size, difference):
    return [(i, i ^ difference) for i in range(size)]


def factor_over_devices(place, keep, send, scale):
    tm, pts = lax.axis_size("tm"), lax.axis_size("pts")
    part = f32(2, 32, 128)
    got = lax.ppermute(send, "tm", xor_pairs(tm, 1))
    parts = call(core_sum_kernel, (part,) * SIDE, [], [place, keep, got])
    parts = [lax.ppermute(parts[d], "pts", xor_pairs(pts, d)) for d in reversed(range(1, SIDE))] + [parts[0]]
    parts = parts[::-1]
    total = call(lambda _, *refs: pair_sum_kernel(*refs), part, [], [place] + parts)
    if pts > SIDE:
        parts = [total] + [lax.ppermute(total, "pts", xor_pairs(pts, d)) for d in range(SIDE, pts, SIDE)]
        total = call(lambda _, *refs: pair_sum_kernel(*refs), part, [], [place] + parts)
    parts = [total] + [lax.ppermute(total, "tm", xor_pairs(tm, d)) for d in range(2, tm, 2)]
    own = call(functools.partial(factor_kernel, scale=scale), part, [], [place] + parts)
    own = [own] + [lax.ppermute(own, "pts", xor_pairs(pts, d)) for d in range(1, SIDE)]
    return own + [lax.ppermute(piece, "tm", xor_pairs(tm, 1)) for piece in own]


def shards(snapshots, weights):
    tm, pts = lax.axis_size("tm"), lax.axis_size("pts")
    me = lax.axis_index("tm")
    points = weights.shape[0]
    scale = 1.0 / (points * tm * pts)

    def piece_of(array, d, start, size):
        return lax.dynamic_slice_in_dim(array, (me ^ d) * points + start, size, 1)

    def exchanged(piece, d):
        return lax.ppermute(piece, "tm", xor_pairs(tm, d))

    last = max(128, points // 4 // 128 * 128)
    body = points - last
    parted = {tm // 2: tm - 1, 3 * tm // 4: tm - 1}
    pieces = {}
    farthest = tm - 1
    sent = piece_of(snapshots, farthest, 0, points)
    rest, sent = lax.optimization_barrier((snapshots, sent))
    pieces[farthest, 0] = exchanged(sent, farthest)
    for d in reversed(range(farthest)):
        piece = piece_of(rest, d, 0, body if d in parted else points)
        pieces[d, 0] = exchanged(piece, d) if d else piece
    for d, after in parted.items():
        sent = piece_of(rest, d, body, last)
        if after is not None:
            sent, _ = lax.optimization_barrier((sent, pieces[after, 0]))
        pieces[d, body] = exchanged(sent, d)
    root = jnp.sqrt(weights)[None, :]
    table_t = jnp.asarray(fourier_table().T)
    place = jnp.stack([me, lax.axis_index("pts")]).astype(jnp.int32)
    half = f32(SIDE, 2, 32, 128)
    spec, keep, send = call(
        functools.partial(spectrum_kernel, places=tuple(pieces)),
        (f32(SEG, 32, points), half, half),
        [pltpu.VMEM((NT, points), jnp.float32)],
        [place, table_t, root, *pieces.values()],
    )
    factors = factor_over_devices(place, keep, send, scale)
    tiles = points // 128
    modes, triangle = call(
        apply_kernel,
        (f32(NF, NB, tiles * 2, 128), f32(2, NF, NB, NB)),
        [pltpu.VMEM((NF, NB, tiles * 2, 128), jnp.float32), pltpu.SemaphoreType.DMA((NF,))],
        [place] + factors + [spec],
        [pl.ANY, pltpu.VMEM],
    )
    modes = modes.reshape(NF, NB, tiles, 2, 128).transpose(3, 0, 1, 2, 4).reshape(2, NF, NB, points)
    return (modes, triangle)


def solution(mesh):
    placed = (P("tm", "pts"), P(("pts", "tm")))
    return jax.shard_map(
        shards,
        mesh=mesh,
        in_specs=placed,
        out_specs=(P(None, None, None, ("pts", "tm")), P()),
        check_vma=False,
    )
```

```python
import functools
import math

import jax
import jax.numpy as jnp
import numpy as np
from jax import lax
from jax.experimental import pallas as pl
from jax.experimental.pallas import tpu as pltpu
from jax.sharding import PartitionSpec as P

SEG = 64
HOP = 32
NF = 33
NT = 1024
NB = 31
SLOTS = 32
GROUPS = 8
SIDE = 4
CUTS = 4
VMEM_BYTES = 24 * 1024 * 1024


def fourier_table():
    sample = np.arange(SEG, dtype=np.float64)[:, None]
    column = np.arange(SEG)[None, :]
    frequency = np.where(column < NF, column, column - HOP).astype(np.float64)
    window = 0.5 - 0.5 * np.cos(2.0 * math.pi * sample / SEG)
    phase_angle = 2.0 * math.pi * frequency * sample / SEG
    waveform = np.where(column < NF, np.cos(phase_angle), -np.sin(phase_angle))
    return (waveform * window / math.sqrt(3 * SEG / 8)).astype(np.float32)


def slices_of(value, count):
    parts = []
    for number in range(count):
        part = value.astype(jnp.bfloat16)
        parts.append(part)
        if number + 1 < count:
            value = value - part.astype(jnp.float32)
    return parts


def two_sum(a, b):
    total = a + b
    rest = total - a
    return total, (a - (total - rest)) + (b - rest)


def pair_add(a, b):
    high, low = two_sum(a[0], b[0])
    low = low + (a[1] + b[1])
    total = high + low
    return total, low - (total - high)


def pair_tree(values):
    while len(values) > 1:
        values = [pair_add(values[i], values[i + 1]) for i in range(0, len(values), 2)]
    return values[0]


def halves(a):
    shifted = a * 4097.0
    high = shifted - (shifted - a)
    return high, a - high


def pair_product(a, a_halves, b, b_halves):
    product = a[0] * b[0]
    (ah, al), (bh, bl) = a_halves, b_halves
    error = ((ah * bh - product) + ah * bl + al * bh) + al * bl
    return product, error + (a[0] * b[1] + a[1] * b[0])


def spectrum_body(table_t, records, spec_ref):
    halves_t = jnp.concatenate([table_t[:, :HOP], table_t[:, HOP:]], axis=0)
    t1, t2, t3 = slices_of(halves_t, 3)
    left = jnp.concatenate([t1, t1, t1, t2, t2, t3], axis=1)
    x1, x2, x3 = slices_of(records, 3)
    before = None
    for hop in range(NT // HOP):
        at = slice(HOP * hop, HOP * hop + HOP)
        right = jnp.concatenate([x1[at], x2[at], x3[at], x1[at], x2[at], x1[at]], axis=0)
        out = jnp.dot(left, right, preferred_element_type=jnp.float32)
        if hop:
            spec_ref[:, hop - 1, :] = before + out[SEG:]
        before = out[:SEG]
    spec_ref[:, NB, :] = jnp.zeros((SEG, records.shape[1]), jnp.float32)


def cut_rows(real, imag):
    top = jnp.maximum(jnp.max(jnp.abs(real), axis=1, keepdims=True), jnp.max(jnp.abs(imag), axis=1, keepdims=True))
    grid = top * (1.5 * 2.0**17)
    cuts = []
    for _ in range(CUTS):
        cut = ((real + grid) - grid, (imag + grid) - grid)
        real, imag = real - cut[0], imag - cut[1]
        grid = grid * 2.0**-7
        cuts.append(cut)
    return cuts


def gram_products(real, imag):
    rows = jnp.concatenate([part for cut in cut_rows(real, imag) for part in cut], axis=0).astype(jnp.bfloat16)
    return lax.dot_general(rows, rows, (((1,), (1,)), ((), ())), preferred_element_type=jnp.float32)


def gram_pairs(products, two_real):
    lane = lax.broadcasted_iota(jnp.int32, (32, 128), 1)
    is_real = lane // 32 % 2 == 0
    front = lane < 64

    def block(number, half):
        return products[32 * number:32 * number + 32, 128 * half:128 * half + 128]

    def combine(from_real, from_imag):
        swapped = jnp.take_along_axis(from_imag, lane ^ 32, axis=1, mode="promise_in_bounds")
        result = from_real + jnp.where(is_real, swapped, -swapped)
        if two_real is None:
            return result
        return jnp.where(two_real, jnp.where(is_real, from_real, from_imag), result)

    first = combine(block(0, 0), block(1, 0))
    second = combine(block(2, 0), block(3, 0))
    rest_real, rest_imag = (
        block(6 + part, 1) + (block(4 + part, 1) + block(6 + part, 0)) + (block(2 + part, 1) + block(4 + part, 0)) + block(part, 1)
        for part in range(2)
    )
    low = combine(rest_real, rest_imag) + jnp.where(front, 0.0, second)
    low = low[:, :64] + low[:, 64:]
    high, rest = two_sum(first[:, :64], first[:, 64:])
    high, more = two_sum(high, second[:, :64])
    low = low + (rest + more)
    total = high + low
    return total, low - (total - high)


def gram_half(spec_ref, out_ref, side):
    row = lax.broadcasted_iota(jnp.int32, (32, 32), 0)
    column = lax.broadcasted_iota(jnp.int32, (32, 32), 1)

    def products_of(step):
        slot = side * SIDE * 4 + step
        return gram_products(spec_ref[slot], spec_ref[SLOTS + slot])

    ahead = products_of(0)
    for step in range(4 * SIDE):
        products = ahead
        if step + 1 < 4 * SIDE:
            ahead = products_of(step + 1)
        q, s = divmod(step, 4)
        if s == 0:
            packed = [[], []]
        sums = gram_pairs(products, side == 0 if step == 0 else None)
        for part in range(2):
            real, imag = sums[part][:, :32], sums[part][:, 32:]
            square = jnp.where(column >= row, real, imag)
            if step == 0:
                diagonal = jnp.sum(jnp.where(column == row, imag, 0.0), axis=0, keepdims=True)
                square = jnp.where(row == NB, diagonal, square)
            packed[part].append(square)
            if s == 3:
                out_ref[q, part] = jnp.concatenate(packed[part], axis=1)


def spectrum_kernel(table_ref, root_ref, *refs, places):
    pieces, (spec_ref, send_ref, records_ref) = refs[:len(places)], refs[len(places):]
    for (d, first), piece in zip(places, pieces):
        rows, size = piece.shape
        start = pl.multiple_of((lax.axis_index("tm") ^ d) * rows, rows)
        at = slice(first, first + size)
        records_ref[pl.ds(start, rows), at] = piece[...] * root_ref[:, at]
    spectrum_body(table_ref[...], records_ref[...], spec_ref)
    gram_half(spec_ref, send_ref, (lax.axis_index("tm") & 1) ^ 1)


def keep_kernel(spec_ref, keep_ref):
    gram_half(spec_ref, keep_ref, lax.axis_index("tm") & 1)


def core_sum_kernel(keep_ref, got_ref, *out_refs):
    for d in range(SIDE):
        q = (lax.axis_index("pts") & (SIDE - 1)) ^ d
        high, low = pair_add((keep_ref[q, 0], keep_ref[q, 1]), (got_ref[q, 0], got_ref[q, 1]))
        out_refs[d][0] = high
        out_refs[d][1] = low


def pair_sum_kernel(*refs):
    high, low = pair_tree([(ref[0], ref[1]) for ref in refs[:-1]])
    refs[-1][0] = high
    refs[-1][1] = low


def swap_squares(square):
    turned = square.T
    return jnp.concatenate([turned[32 * s:32 * s + 32] for s in range(4)], axis=1)


def factor_kernel(*refs, scale):
    out_ref = refs[-1]
    high, low = pair_tree([(ref[0], ref[1]) for ref in refs[:-1]])
    shape = (32, 128)
    row = lax.broadcasted_iota(jnp.int32, shape, 0)
    lane = lax.broadcasted_iota(jnp.int32, shape, 1)
    column = lane % 32
    first = jnp.logical_and((lax.axis_index("tm") & 1) == 0, (lax.axis_index("pts") & (SIDE - 1)) == 0)
    two_real = jnp.logical_and(lane < 32, first)
    sign = jnp.where(two_real, 1.0, -1.0)
    real, imag = [], []
    for square in (high, low):
        turned = swap_squares(square)
        diagonal = jnp.where(two_real, square[NB:NB + 1], 0.0)
        real.append(jnp.where(column >= row, square, turned))
        imag.append(jnp.where(column < row, square, jnp.where(column == row, diagonal, turned * sign)))
    inside = jnp.logical_and(row < NB, column < NB)
    real = [jnp.where(inside, part * scale, 0.0) for part in real]
    imag = [jnp.where(inside, part * scale, 0.0) for part in imag]

    shape = (8, 128)
    row = lax.broadcasted_iota(jnp.int32, shape, 0)
    lane = lax.broadcasted_iota(jnp.int32, shape, 1)
    column = lane % 32
    base = lane - column
    two_real = jnp.logical_and(lane < 32, first)
    real = [[part[8 * i:8 * i + 8] for part in real] for i in range(4)]
    imag = [[part[8 * i:8 * i + 8] for part in imag] for i in range(4)]

    def spread(value, at):
        return jnp.take_along_axis(value, base + at, axis=1, mode="promise_in_bounds")

    def quotient(value, pivot, pivot_halves, inverse):
        first_part = value[0] * inverse
        product, error = pair_product((first_part, 0.0), halves(first_part), (pivot[0], 0.0), pivot_halves)
        rest = ((value[0] - product) - error) + (value[1] - first_part * pivot[1])
        return first_part, rest * inverse

    def minus(value, products):
        high, low = value[0], value[1]
        for product in products:
            high, error = two_sum(high, -product[0])
            low = low + (error - product[1])
        total = high + low
        return [total, low - (total - high)]

    for k in range(NB):
        at = k % 8
        line_real = [jnp.broadcast_to(part[at:at + 1], shape) for part in real[k // 8]]
        line_imag = [jnp.broadcast_to(part[at:at + 1], shape) for part in imag[k // 8]]
        pivot_real = [spread(part, k) for part in line_real]
        pivot_imag = [jnp.where(two_real, spread(part, k), own) for part, own in zip(line_imag, pivot_real)]
        real_halves, imag_halves = halves(pivot_real[0]), halves(pivot_imag[0])
        real_inverse = 1.0 / pivot_real[0]
        imag_inverse = jnp.where(two_real, 1.0 / pivot_imag[0], real_inverse)
        here = column == k
        line_real = (jnp.where(here, 1.0, line_real[0]), jnp.where(here, 0.0, line_real[1]))
        line_imag = (
            jnp.where(here, jnp.where(two_real, 1.0, 0.0), line_imag[0]),
            jnp.where(here, 0.0, line_imag[1]),
        )
        line_real_halves, line_imag_halves = halves(line_real[0]), halves(line_imag[0])
        for i in range((k + 1) // 8, 4):
            some = 8 * i <= k
            below = row > k - 8 * i
            step_real = [spread(part, k) for part in real[i]]
            step_imag = [spread(part, k) for part in imag[i]]
            if some:
                step_real = [jnp.where(below, part, 0.0) for part in step_real]
                step_imag = [jnp.where(below, part, 0.0) for part in step_imag]
            step_real = quotient(step_real, pivot_real, real_halves, real_inverse)
            step_imag = quotient(step_imag, pivot_imag, imag_halves, imag_inverse)
            cross = tuple(jnp.where(two_real, 0.0, part) for part in step_imag)
            own = tuple(jnp.where(two_real, b, a) for a, b in zip(step_real, step_imag))
            clear = jnp.logical_and(below, here) if some else here
            block_real = [jnp.where(clear, 0.0, part) for part in real[i]]
            block_imag = [jnp.where(clear, 0.0, part) for part in imag[i]]
            step_halves, cross_halves, own_halves = halves(step_real[0]), halves(cross[0]), halves(own[0])
            p = pair_product(step_real, step_halves, line_real, line_real_halves)
            q = pair_product(cross, cross_halves, line_imag, line_imag_halves)
            real[i] = minus(block_real, [p, (-q[0], -q[1])])
            p = pair_product(own, own_halves, line_imag, line_imag_halves)
            q = pair_product(cross, cross_halves, line_real, line_real_halves)
            imag[i] = minus(block_imag, [p, q])
    for i in range(4):
        at = slice(8 * i, 8 * i + 8)
        pivot_real = spread(real[i][0], row + 8 * i)
        pivot_imag = jnp.where(two_real, spread(imag[i][0], row + 8 * i), pivot_real)
        good = row + 8 * i < NB
        out_ref[0, at] = jnp.where(good, real[i][0] / jnp.sqrt(pivot_real), 0.0)
        out_ref[1, at] = jnp.where(good, imag[i][0] / jnp.sqrt(pivot_imag), 0.0)


def apply_kernel(*refs):
    pieces, (spec_ref, modes_ref, triangle_ref, tiles_ref, sent) = refs[:GROUPS], refs[GROUPS:]
    points = spec_ref.shape[-1]
    shape = (32, 128)
    row = lax.broadcasted_iota(jnp.int32, shape, 0)
    lane = lax.broadcasted_iota(jnp.int32, shape, 1)
    column = lane % 32
    here = column == row
    even = lane // 32 % 2 == 0
    wide = lax.broadcasted_iota(jnp.int32, (64, 128), 1) < 64
    nothing = jnp.zeros((32, 128), jnp.float32)
    copies = []

    def put(frequency, real, imag):
        rows = []
        for tile in range(points // 128):
            at = slice(128 * tile, 128 * tile + 128)
            rows += [real[:, at], nothing if imag is None else imag[:, at]]
        number = len(copies)
        tiles_ref[number] = jnp.swapaxes(jnp.stack(rows, axis=0), 0, 1)[:NB]
        copy = pltpu.make_async_copy(tiles_ref.at[number], modes_ref.at[frequency], sent.at[number])
        copy.start()
        copies.append(copy)

    last_real = jnp.zeros((32, points), jnp.float32)
    last_triangle = jnp.zeros((NB, NB), jnp.float32)
    for c in range(2):
        for d in range(SIDE):
            piece = pieces[SIDE * c + d]
            group = ((lax.axis_index("tm") & 1) ^ c) * SIDE + ((lax.axis_index("pts") & (SIDE - 1)) ^ d)
            is_first = group == 0
            both_real, both_imag = piece[0], piece[1]
            upper_real = jnp.where(column >= row, both_real, 0.0)
            upper_imag = jnp.where(column >= row, both_imag, 0.0)
            two_real = jnp.logical_and(lane < 32, is_first)
            low_real = jnp.where(column < row, both_real, jnp.where(here, 1.0 / both_real, 0.0))
            low_imag = jnp.where(
                column < row, both_imag, jnp.where(jnp.logical_and(here, two_real), 1.0 / both_imag, 0.0)
            )
            good = row < NB
            low_real = jnp.where(good, low_real, 0.0)
            low_imag = jnp.where(good, low_imag, 0.0)
            cross = jnp.where(two_real, 0.0, low_imag)
            own = jnp.where(two_real, low_imag, low_real)
            for s in range(4):
                slot = 4 * group + s

                def spread(value):
                    return jnp.take_along_axis(value, 32 * s + column, axis=1, mode="promise_in_bounds")

                wide_cross = spread(cross)
                top = jnp.where(even, spread(low_real), wide_cross)
                bottom = jnp.where(even, -wide_cross, spread(own))
                l0, l1, l2 = (part.astype(jnp.float32) for part in slices_of(jnp.concatenate([top, bottom], axis=0), 3))
                left = [l0, jnp.where(wide, l1, l0), jnp.where(wide, l1, l2)]
                left = jnp.concatenate([part.astype(jnp.bfloat16) for part in left], axis=1)
                r0, r1, r2 = slices_of(jnp.concatenate([spec_ref[slot], spec_ref[SLOTS + slot]], axis=0), 3)
                right = jnp.concatenate([r0, r1, r0, r2, r1, r0], axis=0)
                out = jnp.dot(left, right, preferred_element_type=jnp.float32)
                real, imag = out[:32], out[32:]
                square = upper_imag[:NB, 32 * s:32 * s + NB]
                if s == 0:
                    last_real = jnp.where(is_first, imag, last_real)
                    last_triangle = jnp.where(is_first, square, last_triangle)
                    imag = jnp.where(is_first, 0.0, imag)
                    square = jnp.where(is_first, 0.0, square)
                put(slot, real, imag)
                triangle_ref[0, slot] = upper_real[:NB, 32 * s:32 * s + NB]
                triangle_ref[1, slot] = square
    put(SLOTS, last_real, None)
    triangle_ref[0, SLOTS] = last_triangle
    triangle_ref[1, SLOTS] = jnp.zeros((NB, NB), jnp.float32)
    for copy in copies:
        copy.wait()


def call(body, out_shape, scratch, operands, out_spaces=None):
    vmem = pl.BlockSpec(memory_space=pltpu.VMEM)
    return pl.pallas_call(
        body,
        out_shape=out_shape,
        in_specs=[vmem] * len(operands),
        out_specs=[pl.BlockSpec(memory_space=space) for space in out_spaces] if out_spaces else jax.tree.map(lambda _: vmem, out_shape),
        scratch_shapes=scratch,
        compiler_params=pltpu.CompilerParams(vmem_limit_bytes=VMEM_BYTES),
    )(*operands)


def f32(*shape):
    return jax.ShapeDtypeStruct(shape, jnp.float32)


def xor_pairs(size, difference):
    return [(i, i ^ difference) for i in range(size)]


def factor_over_devices(keep, got, scale):
    tm, pts = lax.axis_size("tm"), lax.axis_size("pts")
    part = f32(2, 32, 128)
    parts = call(core_sum_kernel, (part,) * SIDE, [], [keep, got])
    parts = [lax.ppermute(parts[d], "pts", xor_pairs(pts, d)) for d in reversed(range(1, SIDE))] + [parts[0]]
    parts = parts[::-1]
    total = call(pair_sum_kernel, part, [], parts)
    if pts > SIDE:
        parts = [total] + [lax.ppermute(total, "pts", xor_pairs(pts, d)) for d in range(SIDE, pts, SIDE)]
        total = call(pair_sum_kernel, part, [], parts)
    parts = [total] + [lax.ppermute(total, "tm", xor_pairs(tm, d)) for d in range(2, tm, 2)]
    own = call(functools.partial(factor_kernel, scale=scale), part, [], parts)
    own = [own] + [lax.ppermute(own, "pts", xor_pairs(pts, d)) for d in range(1, SIDE)]
    return own + [lax.ppermute(piece, "tm", xor_pairs(tm, 1)) for piece in own]


def shards(snapshots, weights):
    tm, pts = lax.axis_size("tm"), lax.axis_size("pts")
    me = lax.axis_index("tm")
    points = weights.shape[0]
    scale = 1.0 / (points * tm * pts)

    def piece_of(array, d, start, size):
        return lax.dynamic_slice_in_dim(array, (me ^ d) * points + start, size, 1)

    def exchanged(piece, d):
        return lax.ppermute(piece, "tm", xor_pairs(tm, d))

    last = max(128, points // 4 // 128 * 128)
    body = points - last
    parted = {tm // 2: tm - 1, 3 * tm // 4: tm - 1}
    pieces = {}
    farthest = tm - 1
    sent = piece_of(snapshots, farthest, 0, points)
    rest, sent = lax.optimization_barrier((snapshots, sent))
    pieces[farthest, 0] = exchanged(sent, farthest)
    for d in reversed(range(farthest)):
        piece = piece_of(rest, d, 0, body if d in parted else points)
        pieces[d, 0] = exchanged(piece, d) if d else piece
    for d, after in parted.items():
        sent = piece_of(rest, d, body, last)
        if after is not None:
            sent, _ = lax.optimization_barrier((sent, pieces[after, 0]))
        pieces[d, body] = exchanged(sent, d)
    root = jnp.sqrt(weights)[None, :]
    table_t = jnp.asarray(fourier_table().T)
    half = f32(SIDE, 2, 32, 128)
    spec, send = call(
        functools.partial(spectrum_kernel, places=tuple(pieces)),
        (f32(SEG, 32, points), half),
        [pltpu.VMEM((NT, points), jnp.float32)],
        [table_t, root, *pieces.values()],
    )
    got = lax.ppermute(send, "tm", xor_pairs(tm, 1))
    keep = call(keep_kernel, half, [], [spec])
    factors = factor_over_devices(keep, got, scale)
    tiles = points // 128
    modes, triangle = call(
        apply_kernel,
        (f32(NF, NB, tiles * 2, 128), f32(2, NF, NB, NB)),
        [pltpu.VMEM((NF, NB, tiles * 2, 128), jnp.float32), pltpu.SemaphoreType.DMA((NF,))],
        factors + [spec],
        [pl.ANY, pltpu.VMEM],
    )
    modes = modes.reshape(NF, NB, tiles, 2, 128).transpose(3, 0, 1, 2, 4).reshape(2, NF, NB, points)
    return (modes, triangle)


def solution(mesh):
    placed = (P("tm", "pts"), P(("pts", "tm")))
    return jax.shard_map(
        shards,
        mesh=mesh,
        in_specs=placed,
        out_specs=(P(None, None, None, ("pts", "tm")), P()),
        check_vma=False,
    )
```

```python
import functools
import math

import jax
import jax.numpy as jnp
import numpy as np
from jax import lax
from jax.experimental import pallas as pl
from jax.experimental.pallas import tpu as pltpu
from jax.sharding import PartitionSpec as P

SEG = 64
HOP = 32
NF = 33
NT = 1024
NB = 31
SLOTS = 32
GROUPS = 8
SIDE = 4
CUTS = 4
VMEM_BYTES = 24 * 1024 * 1024


def fourier_table():
    sample = np.arange(SEG, dtype=np.float64)[:, None]
    column = np.arange(SEG)[None, :]
    frequency = np.where(column < NF, column, column - HOP).astype(np.float64)
    window = 0.5 - 0.5 * np.cos(2.0 * math.pi * sample / SEG)
    phase_angle = 2.0 * math.pi * frequency * sample / SEG
    waveform = np.where(column < NF, np.cos(phase_angle), -np.sin(phase_angle))
    return (waveform * window / math.sqrt(3 * SEG / 8)).astype(np.float32)


def slices_of(value, count):
    parts = []
    for number in range(count):
        part = value.astype(jnp.bfloat16)
        parts.append(part)
        if number + 1 < count:
            value = value - part.astype(jnp.float32)
    return parts


def two_sum(a, b):
    total = a + b
    rest = total - a
    return total, (a - (total - rest)) + (b - rest)


def pair_add(a, b):
    high, low = two_sum(a[0], b[0])
    low = low + (a[1] + b[1])
    total = high + low
    return total, low - (total - high)


def pair_tree(values):
    while len(values) > 1:
        values = [pair_add(values[i], values[i + 1]) for i in range(0, len(values), 2)]
    return values[0]


def halves(a):
    shifted = a * 4097.0
    high = shifted - (shifted - a)
    return high, a - high


def pair_product(a, a_halves, b, b_halves):
    product = a[0] * b[0]
    (ah, al), (bh, bl) = a_halves, b_halves
    error = ((ah * bh - product) + ah * bl + al * bh) + al * bl
    return product, error + (a[0] * b[1] + a[1] * b[0])


def spectrum_body(table_t, records, spec_ref):
    halves_t = jnp.concatenate([table_t[:, :HOP], table_t[:, HOP:]], axis=0)
    t1, t2, t3 = slices_of(halves_t, 3)
    left = jnp.concatenate([t1, t1, t1, t2, t2, t3], axis=1)
    x1, x2, x3 = slices_of(records, 3)
    before = None
    for hop in range(NT // HOP):
        at = slice(HOP * hop, HOP * hop + HOP)
        right = jnp.concatenate([x1[at], x2[at], x3[at], x1[at], x2[at], x1[at]], axis=0)
        out = jnp.dot(left, right, preferred_element_type=jnp.float32)
        if hop:
            spec_ref[:, hop - 1, :] = before + out[SEG:]
        before = out[:SEG]
    spec_ref[:, NB, :] = jnp.zeros((SEG, records.shape[1]), jnp.float32)


def cut_rows(real, imag):
    top = jnp.maximum(jnp.max(jnp.abs(real), axis=1, keepdims=True), jnp.max(jnp.abs(imag), axis=1, keepdims=True))
    grid = top * (1.5 * 2.0**17)
    cuts = []
    for _ in range(CUTS):
        cut = ((real + grid) - grid, (imag + grid) - grid)
        real, imag = real - cut[0], imag - cut[1]
        grid = grid * 2.0**-7
        cuts.append(cut)
    return cuts


def gram_products(real, imag):
    rows = jnp.concatenate([part for cut in cut_rows(real, imag) for part in cut], axis=0).astype(jnp.bfloat16)
    return lax.dot_general(rows, rows, (((1,), (1,)), ((), ())), preferred_element_type=jnp.float32)


def gram_pairs(products, two_real):
    lane = lax.broadcasted_iota(jnp.int32, (32, 128), 1)
    is_real = lane // 32 % 2 == 0
    front = lane < 64

    def block(number, half):
        return products[32 * number:32 * number + 32, 128 * half:128 * half + 128]

    def combine(from_real, from_imag):
        swapped = jnp.take_along_axis(from_imag, lane ^ 32, axis=1, mode="promise_in_bounds")
        result = from_real + jnp.where(is_real, swapped, -swapped)
        if two_real is None:
            return result
        return jnp.where(two_real, jnp.where(is_real, from_real, from_imag), result)

    first = combine(block(0, 0), block(1, 0))
    second = combine(block(2, 0), block(3, 0))
    rest_real, rest_imag = (
        block(6 + part, 1) + (block(4 + part, 1) + block(6 + part, 0)) + (block(2 + part, 1) + block(4 + part, 0)) + block(part, 1)
        for part in range(2)
    )
    low = combine(rest_real, rest_imag) + jnp.where(front, 0.0, second)
    low = low[:, :64] + low[:, 64:]
    high, rest = two_sum(first[:, :64], first[:, 64:])
    high, more = two_sum(high, second[:, :64])
    low = low + (rest + more)
    total = high + low
    return total, low - (total - high)


def group_at(other_core, d):
    return ((lax.axis_index("tm") & 1) ^ other_core) * SIDE + ((lax.axis_index("pts") & (SIDE - 1)) ^ d)


def gram_groups(spec_ref, groups):
    row = lax.broadcasted_iota(jnp.int32, (32, 32), 0)
    column = lax.broadcasted_iota(jnp.int32, (32, 32), 1)

    def products_of(step):
        slot = groups[step // 4] * 4 + step % 4
        return gram_products(spec_ref[slot], spec_ref[SLOTS + slot])

    results = []
    ahead = products_of(0)
    for step in range(4 * len(groups)):
        products = ahead
        if step + 1 < 4 * len(groups):
            ahead = products_of(step + 1)
        s = step % 4
        if s == 0:
            packed = [[], []]
        sums = gram_pairs(products, None if s else groups[step // 4] == 0)
        for part in range(2):
            real, imag = sums[part][:, :32], sums[part][:, 32:]
            square = jnp.where(column >= row, real, imag)
            if s == 0:
                diagonal = jnp.sum(jnp.where(column == row, imag, 0.0), axis=0, keepdims=True)
                square = jnp.where(row == NB, diagonal, square)
            packed[part].append(square)
        if s == 3:
            results.append([jnp.concatenate(part, axis=1) for part in packed])
    return results


def spectrum_kernel(table_ref, root_ref, *refs, places):
    pieces, (spec_ref, send_ref, records_ref) = refs[:len(places)], refs[len(places):]
    for (d, first), piece in zip(places, pieces):
        rows, size = piece.shape
        start = pl.multiple_of((lax.axis_index("tm") ^ d) * rows, rows)
        at = slice(first, first + size)
        records_ref[pl.ds(start, rows), at] = piece[...] * root_ref[:, at]
    spectrum_body(table_ref[...], records_ref[...], spec_ref)
    for d, pair in enumerate(gram_groups(spec_ref, [group_at(1, d) for d in range(SIDE)])):
        send_ref[d, 0], send_ref[d, 1] = pair


def keep_kernel(spec_ref, keep_ref):
    for number, pair in enumerate(gram_groups(spec_ref, [group_at(0, d) for d in range(1, SIDE)])):
        keep_ref[number, 0], keep_ref[number, 1] = pair


def core_sum_kernel(keep_ref, got_ref, *out_refs):
    for number, out_ref in enumerate(out_refs):
        d = number + 1
        out_ref[0], out_ref[1] = pair_add((keep_ref[number, 0], keep_ref[number, 1]), (got_ref[d, 0], got_ref[d, 1]))


def own_kernel(spec_ref, got_ref, out_ref):
    own = gram_groups(spec_ref, [group_at(0, 0)])[0]
    out_ref[0], out_ref[1] = pair_add(own, (got_ref[0, 0], got_ref[0, 1]))


def pair_sum_kernel(*refs):
    high, low = pair_tree([(ref[0], ref[1]) for ref in refs[:-1]])
    refs[-1][0] = high
    refs[-1][1] = low


def swap_squares(square):
    turned = square.T
    return jnp.concatenate([turned[32 * s:32 * s + 32] for s in range(4)], axis=1)


def factor_kernel(*refs, scale):
    out_ref = refs[-1]
    high, low = pair_tree([(ref[0], ref[1]) for ref in refs[:-1]])
    shape = (32, 128)
    row = lax.broadcasted_iota(jnp.int32, shape, 0)
    lane = lax.broadcasted_iota(jnp.int32, shape, 1)
    column = lane % 32
    first = jnp.logical_and((lax.axis_index("tm") & 1) == 0, (lax.axis_index("pts") & (SIDE - 1)) == 0)
    two_real = jnp.logical_and(lane < 32, first)
    sign = jnp.where(two_real, 1.0, -1.0)
    real, imag = [], []
    for square in (high, low):
        turned = swap_squares(square)
        diagonal = jnp.where(two_real, square[NB:NB + 1], 0.0)
        real.append(jnp.where(column >= row, square, turned))
        imag.append(jnp.where(column < row, square, jnp.where(column == row, diagonal, turned * sign)))
    inside = jnp.logical_and(row < NB, column < NB)
    real = [jnp.where(inside, part * scale, 0.0) for part in real]
    imag = [jnp.where(inside, part * scale, 0.0) for part in imag]

    shape = (8, 128)
    row = lax.broadcasted_iota(jnp.int32, shape, 0)
    lane = lax.broadcasted_iota(jnp.int32, shape, 1)
    column = lane % 32
    base = lane - column
    two_real = jnp.logical_and(lane < 32, first)
    real = [[part[8 * i:8 * i + 8] for part in real] for i in range(4)]
    imag = [[part[8 * i:8 * i + 8] for part in imag] for i in range(4)]

    def spread(value, at):
        return jnp.take_along_axis(value, base + at, axis=1, mode="promise_in_bounds")

    def quotient(value, pivot, pivot_halves, inverse):
        first_part = value[0] * inverse
        product, error = pair_product((first_part, 0.0), halves(first_part), (pivot[0], 0.0), pivot_halves)
        rest = ((value[0] - product) - error) + (value[1] - first_part * pivot[1])
        return first_part, rest * inverse

    def minus(value, products):
        high, low = value[0], value[1]
        for product in products:
            high, error = two_sum(high, -product[0])
            low = low + (error - product[1])
        total = high + low
        return [total, low - (total - high)]

    def pivots(real_part, imag_part):
        return real_part, [jnp.where(two_real, b, a) for a, b in zip(real_part, imag_part)]

    def row_of(blocks, at):
        return [jnp.broadcast_to(part[at % 8:at % 8 + 1], shape) for part in blocks[at // 8]]

    def next_pivots(k):
        next_real, next_imag = row_of(real, k + 1), row_of(imag, k + 1)
        left_real, left_imag = ([spread(part, k) for part in parts] for parts in (next_real, next_imag))
        step_real = quotient(left_real, pivot_real, real_halves, real_inverse)
        step_imag = quotient(left_imag, pivot_imag, imag_halves, imag_inverse)
        p = pair_product(step_real, halves(step_real[0]), left_real, halves(left_real[0]))
        q = pair_product(step_imag, halves(step_imag[0]), left_imag, halves(left_imag[0]))
        cross = [jnp.where(two_real, 0.0, part) for part in q]
        new_real = minus([spread(part, k + 1) for part in next_real], [p, cross])
        new_imag = minus([spread(part, k + 1) for part in next_imag], [q])
        return pivots(new_real, new_imag)

    pivot_real, pivot_imag = pivots([spread(part, 0) for part in row_of(real, 0)], [spread(part, 0) for part in row_of(imag, 0)])
    for k in range(NB):
        at = k % 8
        line_real = [jnp.broadcast_to(part[at:at + 1], shape) for part in real[k // 8]]
        line_imag = [jnp.broadcast_to(part[at:at + 1], shape) for part in imag[k // 8]]
        real_halves, imag_halves = halves(pivot_real[0]), halves(pivot_imag[0])
        real_inverse = 1.0 / pivot_real[0]
        imag_inverse = jnp.where(two_real, 1.0 / pivot_imag[0], real_inverse)
        if k + 1 < NB:
            coming = next_pivots(k)
        here = column == k
        line_real = (jnp.where(here, 1.0, line_real[0]), jnp.where(here, 0.0, line_real[1]))
        line_imag = (
            jnp.where(here, jnp.where(two_real, 1.0, 0.0), line_imag[0]),
            jnp.where(here, 0.0, line_imag[1]),
        )
        line_real_halves, line_imag_halves = halves(line_real[0]), halves(line_imag[0])
        for i in range((k + 1) // 8, 4):
            some = 8 * i <= k
            below = row > k - 8 * i
            step_real = [spread(part, k) for part in real[i]]
            step_imag = [spread(part, k) for part in imag[i]]
            if some:
                step_real = [jnp.where(below, part, 0.0) for part in step_real]
                step_imag = [jnp.where(below, part, 0.0) for part in step_imag]
            step_real = quotient(step_real, pivot_real, real_halves, real_inverse)
            step_imag = quotient(step_imag, pivot_imag, imag_halves, imag_inverse)
            cross = tuple(jnp.where(two_real, 0.0, part) for part in step_imag)
            own = tuple(jnp.where(two_real, b, a) for a, b in zip(step_real, step_imag))
            clear = jnp.logical_and(below, here) if some else here
            block_real = [jnp.where(clear, 0.0, part) for part in real[i]]
            block_imag = [jnp.where(clear, 0.0, part) for part in imag[i]]
            step_halves, cross_halves, own_halves = halves(step_real[0]), halves(cross[0]), halves(own[0])
            p = pair_product(step_real, step_halves, line_real, line_real_halves)
            q = pair_product(cross, cross_halves, line_imag, line_imag_halves)
            real[i] = minus(block_real, [p, (-q[0], -q[1])])
            p = pair_product(own, own_halves, line_imag, line_imag_halves)
            q = pair_product(cross, cross_halves, line_real, line_real_halves)
            imag[i] = minus(block_imag, [p, q])
        pivot_real, pivot_imag = coming
    for i in range(4):
        at = slice(8 * i, 8 * i + 8)
        pivot_real = spread(real[i][0], row + 8 * i)
        pivot_imag = jnp.where(two_real, spread(imag[i][0], row + 8 * i), pivot_real)
        good = row + 8 * i < NB
        out_ref[0, at] = jnp.where(good, real[i][0] / jnp.sqrt(pivot_real), 0.0)
        out_ref[1, at] = jnp.where(good, imag[i][0] / jnp.sqrt(pivot_imag), 0.0)


def apply_kernel(*refs, side):
    pieces, spec_ref = refs[:SIDE], refs[SIDE]
    if side == 0:
        modes_ref, last_ref, tiles_ref, sent = refs[SIDE + 1:]
    else:
        others, before_ref, _, modes_ref, triangle_ref, tiles_ref, sent = refs[SIDE + 1:2 * SIDE + 1], *refs[2 * SIDE + 1:]
    points = spec_ref.shape[-1]
    shape = (32, 128)
    row = lax.broadcasted_iota(jnp.int32, shape, 0)
    lane = lax.broadcasted_iota(jnp.int32, shape, 1)
    column = lane % 32
    here = column == row
    even = lane // 32 % 2 == 0
    wide = lax.broadcasted_iota(jnp.int32, (64, 128), 1) < 64
    nothing = jnp.zeros((32, 128), jnp.float32)
    copies = []

    def put(frequency, real, imag):
        rows = []
        for tile in range(points // 128):
            at = slice(128 * tile, 128 * tile + 128)
            rows += [real[:, at], nothing if imag is None else imag[:, at]]
        number = len(copies)
        tiles_ref[number] = jnp.swapaxes(jnp.stack(rows, axis=0), 0, 1)[:NB]
        copy = pltpu.make_async_copy(tiles_ref.at[number], modes_ref.at[frequency], sent.at[number])
        copy.start()
        copies.append(copy)

    def group_of(c, d):
        return ((lax.axis_index("tm") & 1) ^ c) * SIDE + ((lax.axis_index("pts") & (SIDE - 1)) ^ d)

    last_real = jnp.zeros((32, points), jnp.float32) if side == 0 else before_ref[...]
    for d in range(SIDE):
        piece = pieces[d]
        group = group_of(side, d)
        is_first = group == 0
        both_real, both_imag = piece[0], piece[1]
        two_real = jnp.logical_and(lane < 32, is_first)
        low_real = jnp.where(column < row, both_real, jnp.where(here, 1.0 / both_real, 0.0))
        low_imag = jnp.where(
            column < row, both_imag, jnp.where(jnp.logical_and(here, two_real), 1.0 / both_imag, 0.0)
        )
        good = row < NB
        low_real = jnp.where(good, low_real, 0.0)
        low_imag = jnp.where(good, low_imag, 0.0)
        cross = jnp.where(two_real, 0.0, low_imag)
        own = jnp.where(two_real, low_imag, low_real)
        for s in range(4):
            slot = 4 * group + s

            def spread(value):
                return jnp.take_along_axis(value, 32 * s + column, axis=1, mode="promise_in_bounds")

            wide_cross = spread(cross)
            top = jnp.where(even, spread(low_real), wide_cross)
            bottom = jnp.where(even, -wide_cross, spread(own))
            l0, l1, l2 = (part.astype(jnp.float32) for part in slices_of(jnp.concatenate([top, bottom], axis=0), 3))
            left = [l0, jnp.where(wide, l1, l0), jnp.where(wide, l1, l2)]
            left = jnp.concatenate([part.astype(jnp.bfloat16) for part in left], axis=1)
            r0, r1, r2 = slices_of(jnp.concatenate([spec_ref[slot], spec_ref[SLOTS + slot]], axis=0), 3)
            right = jnp.concatenate([r0, r1, r0, r2, r1, r0], axis=0)
            out = jnp.dot(left, right, preferred_element_type=jnp.float32)
            real, imag = out[:32], out[32:]
            if s == 0:
                last_real = jnp.where(is_first, imag, last_real)
                imag = jnp.where(is_first, 0.0, imag)
            put(slot, real, imag)
    if side == 0:
        last_ref[...] = last_real
    else:
        put(SLOTS, last_real, None)
        last_triangle = jnp.zeros((NB, NB), jnp.float32)
        for c, parts in ((0, others), (1, pieces)):
            for d, piece in enumerate(parts):
                group = group_of(c, d)
                upper_real = jnp.where(column >= row, piece[0], 0.0)
                upper_imag = jnp.where(column >= row, piece[1], 0.0)
                for s in range(4):
                    square = upper_imag[:NB, 32 * s:32 * s + NB]
                    if s == 0:
                        last_triangle = jnp.where(group == 0, square, last_triangle)
                        square = jnp.where(group == 0, 0.0, square)
                    triangle_ref[0, 4 * group + s] = upper_real[:NB, 32 * s:32 * s + NB]
                    triangle_ref[1, 4 * group + s] = square
        triangle_ref[0, SLOTS] = last_triangle
        triangle_ref[1, SLOTS] = jnp.zeros((NB, NB), jnp.float32)
    for copy in copies:
        copy.wait()


def call(body, out_shape, scratch, operands, out_spaces=None, aliases=None):
    vmem = pl.BlockSpec(memory_space=pltpu.VMEM)
    return pl.pallas_call(
        body,
        out_shape=out_shape,
        in_specs=[
            pl.BlockSpec(memory_space=pl.ANY) if number in (aliases or {}) else vmem
            for number in range(len(operands))
        ],
        input_output_aliases=aliases or {},
        out_specs=[pl.BlockSpec(memory_space=space) for space in out_spaces] if out_spaces else jax.tree.map(lambda _: vmem, out_shape),
        scratch_shapes=scratch,
        compiler_params=pltpu.CompilerParams(vmem_limit_bytes=VMEM_BYTES),
    )(*operands)


def f32(*shape):
    return jax.ShapeDtypeStruct(shape, jnp.float32)


def xor_pairs(size, difference):
    return [(i, i ^ difference) for i in range(size)]


def factor_over_devices(spec, got, scale):
    tm, pts = lax.axis_size("tm"), lax.axis_size("pts")
    part = f32(2, 32, 128)
    keep = call(keep_kernel, f32(SIDE - 1, 2, 32, 128), [], [spec])
    parts = call(core_sum_kernel, (part,) * (SIDE - 1), [], [keep, got])
    parts = [lax.ppermute(parts[d - 1], "pts", xor_pairs(pts, d)) for d in range(SIDE - 1, 0, -1)]
    parts = [call(own_kernel, part, [], [spec, got])] + parts
    total = call(pair_sum_kernel, part, [], parts)
    if pts > SIDE:
        parts = [total] + [lax.ppermute(total, "pts", xor_pairs(pts, d)) for d in range(SIDE, pts, SIDE)]
        total = call(pair_sum_kernel, part, [], parts)
    parts = [total] + [lax.ppermute(total, "tm", xor_pairs(tm, d)) for d in range(2, tm, 2)]
    own = call(functools.partial(factor_kernel, scale=scale), part, [], parts)
    own = [own] + [lax.ppermute(own, "pts", xor_pairs(pts, d)) for d in range(1, SIDE)]
    return own + [lax.ppermute(piece, "tm", xor_pairs(tm, 1)) for piece in own]


def shards(snapshots, weights):
    tm, pts = lax.axis_size("tm"), lax.axis_size("pts")
    me = lax.axis_index("tm")
    points = weights.shape[0]
    scale = 1.0 / (points * tm * pts)

    def piece_of(array, d, start, size):
        return lax.dynamic_slice_in_dim(array, (me ^ d) * points + start, size, 1)

    def exchanged(piece, d):
        return lax.ppermute(piece, "tm", xor_pairs(tm, d))

    last = max(128, points // 4 // 128 * 128)
    body = points - last
    parted = {tm // 2: tm - 1, 3 * tm // 4: tm - 1}
    pieces = {}
    farthest = tm - 1
    sent = piece_of(snapshots, farthest, 0, points)
    rest, sent = lax.optimization_barrier((snapshots, sent))
    pieces[farthest, 0] = exchanged(sent, farthest)
    for d in reversed(range(farthest)):
        piece = piece_of(rest, d, 0, body if d in parted else points)
        pieces[d, 0] = exchanged(piece, d) if d else piece
    for d, after in parted.items():
        sent = piece_of(rest, d, body, last)
        if after is not None:
            sent, _ = lax.optimization_barrier((sent, pieces[after, 0]))
        pieces[d, body] = exchanged(sent, d)
    root = jnp.sqrt(weights)[None, :]
    table_t = jnp.asarray(fourier_table().T)
    half = f32(SIDE, 2, 32, 128)
    spec, send = call(
        functools.partial(spectrum_kernel, places=tuple(pieces)),
        (f32(SEG, 32, points), half),
        [pltpu.VMEM((NT, points), jnp.float32)],
        [table_t, root, *pieces.values()],
    )
    got = lax.ppermute(send, "tm", xor_pairs(tm, 1))
    factors = factor_over_devices(spec, got, scale)
    tiles = points // 128
    shape = f32(NF, NB, tiles * 2, 128)
    scratch = [pltpu.VMEM((4 * SIDE + 1, NB, tiles * 2, 128), jnp.float32), pltpu.SemaphoreType.DMA((4 * SIDE + 1,))]
    own, others = factors[:SIDE], factors[SIDE:]
    modes, last_real = call(
        functools.partial(apply_kernel, side=0),
        (shape, f32(32, points)),
        scratch,
        [*own, spec],
        [pl.ANY, pltpu.VMEM],
    )
    modes, triangle = call(
        functools.partial(apply_kernel, side=1),
        (shape, f32(2, NF, NB, NB)),
        scratch,
        [*others, spec, *own, last_real, modes],
        [pl.ANY, pltpu.VMEM],
        {2 * SIDE + 2: 0},
    )
    modes = modes.reshape(NF, NB, tiles, 2, 128).transpose(3, 0, 1, 2, 4).reshape(2, NF, NB, points)
    return (modes, triangle)


def solution(mesh):
    placed = (P("tm", "pts"), P(("pts", "tm")))
    return jax.shard_map(
        shards,
        mesh=mesh,
        in_specs=placed,
        out_specs=(P(None, None, None, ("pts", "tm")), P()),
        check_vma=False,
    )
```

```python
import functools
import math

import jax
import jax.numpy as jnp
import numpy as np
from jax import lax
from jax.experimental import pallas as pl
from jax.experimental.pallas import tpu as pltpu
from jax.sharding import PartitionSpec as P

SEG = 64
HOP = 32
NF = 33
NT = 1024
NB = 31
SLOTS = 32
GROUPS = 8
SIDE = 4
CUTS = 4
VMEM_BYTES = 24 * 1024 * 1024


def fourier_table():
    sample = np.arange(SEG, dtype=np.float64)[:, None]
    column = np.arange(SEG)[None, :]
    frequency = np.where(column < NF, column, column - HOP).astype(np.float64)
    window = 0.5 - 0.5 * np.cos(2.0 * math.pi * sample / SEG)
    phase_angle = 2.0 * math.pi * frequency * sample / SEG
    waveform = np.where(column < NF, np.cos(phase_angle), -np.sin(phase_angle))
    return (waveform * window / math.sqrt(3 * SEG / 8)).astype(np.float32)


def slices_of(value, count):
    parts = []
    for number in range(count):
        part = value.astype(jnp.bfloat16)
        parts.append(part)
        if number + 1 < count:
            value = value - part.astype(jnp.float32)
    return parts


def two_sum(a, b):
    total = a + b
    rest = total - a
    return total, (a - (total - rest)) + (b - rest)


def pair_add(a, b):
    high, low = two_sum(a[0], b[0])
    low = low + (a[1] + b[1])
    total = high + low
    return total, low - (total - high)


def pair_tree(values):
    while len(values) > 1:
        values = [pair_add(values[i], values[i + 1]) for i in range(0, len(values), 2)]
    return values[0]


def halves(a):
    shifted = a * 4097.0
    high = shifted - (shifted - a)
    return high, a - high


def pair_product(a, a_halves, b, b_halves):
    product = a[0] * b[0]
    (ah, al), (bh, bl) = a_halves, b_halves
    error = ((ah * bh - product) + ah * bl + al * bh) + al * bl
    return product, error + (a[0] * b[1] + a[1] * b[0])


def spectrum_body(table_t, records, spec_ref):
    halves_t = jnp.concatenate([table_t[:, :HOP], table_t[:, HOP:]], axis=0)
    t1, t2, t3 = slices_of(halves_t, 3)
    left = jnp.concatenate([t1, t1, t1, t2, t2, t3], axis=1)
    x1, x2, x3 = slices_of(records, 3)
    before = None
    for hop in range(NT // HOP):
        at = slice(HOP * hop, HOP * hop + HOP)
        right = jnp.concatenate([x1[at], x2[at], x3[at], x1[at], x2[at], x1[at]], axis=0)
        out = jnp.dot(left, right, preferred_element_type=jnp.float32)
        if hop:
            spec_ref[:, hop - 1, :] = before + out[SEG:]
        before = out[:SEG]
    spec_ref[:, NB, :] = jnp.zeros((SEG, records.shape[1]), jnp.float32)


def cut_rows(real, imag):
    top = jnp.maximum(jnp.max(jnp.abs(real), axis=1, keepdims=True), jnp.max(jnp.abs(imag), axis=1, keepdims=True))
    grid = top * (1.5 * 2.0**17)
    cuts = []
    for _ in range(CUTS):
        cut = ((real + grid) - grid, (imag + grid) - grid)
        real, imag = real - cut[0], imag - cut[1]
        grid = grid * 2.0**-7
        cuts.append(cut)
    return cuts


def gram_products(real, imag):
    rows = jnp.concatenate([part for cut in cut_rows(real, imag) for part in cut], axis=0).astype(jnp.bfloat16)
    return lax.dot_general(rows, rows, (((1,), (1,)), ((), ())), preferred_element_type=jnp.float32)


def gram_pairs(products, two_real):
    lane = lax.broadcasted_iota(jnp.int32, (32, 128), 1)
    is_real = lane // 32 % 2 == 0
    front = lane < 64

    def block(number, half):
        return products[32 * number:32 * number + 32, 128 * half:128 * half + 128]

    def combine(from_real, from_imag):
        swapped = jnp.take_along_axis(from_imag, lane ^ 32, axis=1, mode="promise_in_bounds")
        result = from_real + jnp.where(is_real, swapped, -swapped)
        if two_real is None:
            return result
        return jnp.where(two_real, jnp.where(is_real, from_real, from_imag), result)

    first = combine(block(0, 0), block(1, 0))
    second = combine(block(2, 0), block(3, 0))
    rest_real, rest_imag = (
        block(6 + part, 1) + (block(4 + part, 1) + block(6 + part, 0)) + (block(2 + part, 1) + block(4 + part, 0)) + block(part, 1)
        for part in range(2)
    )
    low = combine(rest_real, rest_imag) + jnp.where(front, 0.0, second)
    low = low[:, :64] + low[:, 64:]
    high, rest = two_sum(first[:, :64], first[:, 64:])
    high, more = two_sum(high, second[:, :64])
    low = low + (rest + more)
    total = high + low
    return total, low - (total - high)


def group_at(other_core, d):
    return ((lax.axis_index("tm") & 1) ^ other_core) * SIDE + ((lax.axis_index("pts") & (SIDE - 1)) ^ d)


def gram_groups(spec_ref, groups):
    row = lax.broadcasted_iota(jnp.int32, (32, 32), 0)
    column = lax.broadcasted_iota(jnp.int32, (32, 32), 1)

    def products_of(step):
        slot = groups[step // 4] * 4 + step % 4
        return gram_products(spec_ref[slot], spec_ref[SLOTS + slot])

    results = []
    ahead = products_of(0)
    for step in range(4 * len(groups)):
        products = ahead
        if step + 1 < 4 * len(groups):
            ahead = products_of(step + 1)
        s = step % 4
        if s == 0:
            packed = [[], []]
        sums = gram_pairs(products, None if s else groups[step // 4] == 0)
        for part in range(2):
            real, imag = sums[part][:, :32], sums[part][:, 32:]
            square = jnp.where(column >= row, real, imag)
            if s == 0:
                diagonal = jnp.sum(jnp.where(column == row, imag, 0.0), axis=0, keepdims=True)
                square = jnp.where(row == NB, diagonal, square)
            packed[part].append(square)
        if s == 3:
            results.append([jnp.concatenate(part, axis=1) for part in packed])
    return results


def spectrum_kernel(table_ref, root_ref, *refs, places):
    pieces, (spec_ref, send_ref, records_ref) = refs[:len(places)], refs[len(places):]
    for (d, first), piece in zip(places, pieces):
        rows, size = piece.shape
        start = pl.multiple_of((lax.axis_index("tm") ^ d) * rows, rows)
        at = slice(first, first + size)
        records_ref[pl.ds(start, rows), at] = piece[...] * root_ref[:, at]
    spectrum_body(table_ref[...], records_ref[...], spec_ref)
    for d, pair in enumerate(gram_groups(spec_ref, [group_at(1, d) for d in range(SIDE)])):
        send_ref[d, 0], send_ref[d, 1] = pair


def keep_kernel(spec_ref, keep_ref):
    for number, pair in enumerate(gram_groups(spec_ref, [group_at(0, d) for d in range(1, SIDE)])):
        keep_ref[number, 0], keep_ref[number, 1] = pair


def core_sum_kernel(keep_ref, got_ref, *out_refs):
    for number, out_ref in enumerate(out_refs):
        d = number + 1
        out_ref[0], out_ref[1] = pair_add((keep_ref[number, 0], keep_ref[number, 1]), (got_ref[d, 0], got_ref[d, 1]))


def own_kernel(spec_ref, got_ref, out_ref):
    own = gram_groups(spec_ref, [group_at(0, 0)])[0]
    out_ref[0], out_ref[1] = pair_add(own, (got_ref[0, 0], got_ref[0, 1]))


def pair_sum_kernel(*refs):
    high, low = pair_tree([(ref[0], ref[1]) for ref in refs[:-1]])
    refs[-1][0] = high
    refs[-1][1] = low


def swap_squares(square):
    turned = square.T
    return jnp.concatenate([turned[32 * s:32 * s + 32] for s in range(4)], axis=1)


def factor_kernel(*refs, scale):
    out_ref = refs[-1]
    high, low = pair_tree([(ref[0], ref[1]) for ref in refs[:-1]])
    shape = (32, 128)
    row = lax.broadcasted_iota(jnp.int32, shape, 0)
    lane = lax.broadcasted_iota(jnp.int32, shape, 1)
    column = lane % 32
    first = jnp.logical_and((lax.axis_index("tm") & 1) == 0, (lax.axis_index("pts") & (SIDE - 1)) == 0)
    two_real = jnp.logical_and(lane < 32, first)
    sign = jnp.where(two_real, 1.0, -1.0)
    real, imag = [], []
    for square in (high, low):
        turned = swap_squares(square)
        diagonal = jnp.where(two_real, square[NB:NB + 1], 0.0)
        real.append(jnp.where(column >= row, square, turned))
        imag.append(jnp.where(column < row, square, jnp.where(column == row, diagonal, turned * sign)))
    inside = jnp.logical_and(row < NB, column < NB)
    real = [jnp.where(inside, part * scale, 0.0) for part in real]
    imag = [jnp.where(inside, part * scale, 0.0) for part in imag]

    shape = (8, 128)
    row = lax.broadcasted_iota(jnp.int32, shape, 0)
    lane = lax.broadcasted_iota(jnp.int32, shape, 1)
    column = lane % 32
    base = lane - column
    two_real = jnp.logical_and(lane < 32, first)
    real = [[part[8 * i:8 * i + 8] for part in real] for i in range(4)]
    imag = [[part[8 * i:8 * i + 8] for part in imag] for i in range(4)]

    def spread(value, at):
        return jnp.take_along_axis(value, base + at, axis=1, mode="promise_in_bounds")

    def quotient(value, pivot, pivot_halves, inverse):
        first_part = value[0] * inverse
        product, error = pair_product((first_part, 0.0), halves(first_part), (pivot[0], 0.0), pivot_halves)
        rest = ((value[0] - product) - error) + (value[1] - first_part * pivot[1])
        return first_part, rest * inverse

    def minus(value, products):
        high, low = value[0], value[1]
        for product in products:
            high, error = two_sum(high, -product[0])
            low = low + (error - product[1])
        total = high + low
        return [total, low - (total - high)]

    def pivots(real_part, imag_part):
        return real_part, [jnp.where(two_real, b, a) for a, b in zip(real_part, imag_part)]

    def row_of(blocks, at):
        return [jnp.broadcast_to(part[at % 8:at % 8 + 1], shape) for part in blocks[at // 8]]

    def next_pivots(k):
        next_real, next_imag = row_of(real, k + 1), row_of(imag, k + 1)
        left_real, left_imag = ([spread(part, k) for part in parts] for parts in (next_real, next_imag))
        step_real = quotient(left_real, pivot_real, real_halves, real_inverse)
        step_imag = quotient(left_imag, pivot_imag, imag_halves, imag_inverse)
        p = pair_product(step_real, halves(step_real[0]), left_real, halves(left_real[0]))
        q = pair_product(step_imag, halves(step_imag[0]), left_imag, halves(left_imag[0]))
        cross = [jnp.where(two_real, 0.0, part) for part in q]
        new_real = minus([spread(part, k + 1) for part in next_real], [p, cross])
        new_imag = minus([spread(part, k + 1) for part in next_imag], [q])
        return pivots(new_real, new_imag)

    pivot_real, pivot_imag = pivots([spread(part, 0) for part in row_of(real, 0)], [spread(part, 0) for part in row_of(imag, 0)])
    for k in range(NB):
        at = k % 8
        line_real = [jnp.broadcast_to(part[at:at + 1], shape) for part in real[k // 8]]
        line_imag = [jnp.broadcast_to(part[at:at + 1], shape) for part in imag[k // 8]]
        real_halves, imag_halves = halves(pivot_real[0]), halves(pivot_imag[0])
        real_inverse = 1.0 / pivot_real[0]
        imag_inverse = jnp.where(two_real, 1.0 / pivot_imag[0], real_inverse)
        if k + 1 < NB:
            coming = next_pivots(k)
        here = column == k
        line_real = (jnp.where(here, 1.0, line_real[0]), jnp.where(here, 0.0, line_real[1]))
        line_imag = (
            jnp.where(here, jnp.where(two_real, 1.0, 0.0), line_imag[0]),
            jnp.where(here, 0.0, line_imag[1]),
        )
        line_real_halves, line_imag_halves = halves(line_real[0]), halves(line_imag[0])
        for i in range((k + 1) // 8, 4):
            some = 8 * i <= k
            below = row > k - 8 * i
            step_real = [spread(part, k) for part in real[i]]
            step_imag = [spread(part, k) for part in imag[i]]
            if some:
                step_real = [jnp.where(below, part, 0.0) for part in step_real]
                step_imag = [jnp.where(below, part, 0.0) for part in step_imag]
            step_real = quotient(step_real, pivot_real, real_halves, real_inverse)
            step_imag = quotient(step_imag, pivot_imag, imag_halves, imag_inverse)
            cross = tuple(jnp.where(two_real, 0.0, part) for part in step_imag)
            own = tuple(jnp.where(two_real, b, a) for a, b in zip(step_real, step_imag))
            clear = jnp.logical_and(below, here) if some else here
            block_real = [jnp.where(clear, 0.0, part) for part in real[i]]
            block_imag = [jnp.where(clear, 0.0, part) for part in imag[i]]
            step_halves, cross_halves, own_halves = halves(step_real[0]), halves(cross[0]), halves(own[0])
            p = pair_product(step_real, step_halves, line_real, line_real_halves)
            q = pair_product(cross, cross_halves, line_imag, line_imag_halves)
            real[i] = minus(block_real, [p, (-q[0], -q[1])])
            p = pair_product(own, own_halves, line_imag, line_imag_halves)
            q = pair_product(cross, cross_halves, line_real, line_real_halves)
            imag[i] = minus(block_imag, [p, q])
        pivot_real, pivot_imag = coming
    for i in range(4):
        at = slice(8 * i, 8 * i + 8)
        pivot_real = spread(real[i][0], row + 8 * i)
        pivot_imag = jnp.where(two_real, spread(imag[i][0], row + 8 * i), pivot_real)
        good = row + 8 * i < NB
        out_ref[0, at] = jnp.where(good, real[i][0] / jnp.sqrt(pivot_real), 0.0)
        out_ref[1, at] = jnp.where(good, imag[i][0] / jnp.sqrt(pivot_imag), 0.0)


def apply_kernel(*refs, side):
    pieces, spec_ref = refs[:SIDE], refs[SIDE]
    if side == 0:
        modes_ref, last_ref, tiles_ref, sent = refs[SIDE + 1:]
    else:
        others, before_ref, _, modes_ref, triangle_ref, tiles_ref, sent = refs[SIDE + 1:2 * SIDE + 1], *refs[2 * SIDE + 1:]
    points = spec_ref.shape[-1]
    shape = (32, 128)
    row = lax.broadcasted_iota(jnp.int32, shape, 0)
    lane = lax.broadcasted_iota(jnp.int32, shape, 1)
    column = lane % 32
    here = column == row
    even = lane // 32 % 2 == 0
    wide = lax.broadcasted_iota(jnp.int32, (64, 128), 1) < 64
    nothing = jnp.zeros((32, 128), jnp.float32)
    copies = []

    def put(frequency, real, imag):
        rows = []
        for tile in range(points // 128):
            at = slice(128 * tile, 128 * tile + 128)
            rows += [real[:, at], nothing if imag is None else imag[:, at]]
        number = len(copies)
        tiles_ref[number] = jnp.swapaxes(jnp.stack(rows, axis=0), 0, 1)[:NB]
        copy = pltpu.make_async_copy(tiles_ref.at[number], modes_ref.at[frequency], sent.at[number])
        copy.start()
        copies.append(copy)

    def group_of(c, d):
        return ((lax.axis_index("tm") & 1) ^ c) * SIDE + ((lax.axis_index("pts") & (SIDE - 1)) ^ d)

    last_real = jnp.zeros((32, points), jnp.float32) if side == 0 else before_ref[...]
    for d in range(SIDE):
        piece = pieces[d]
        group = group_of(side, d)
        is_first = group == 0
        both_real, both_imag = piece[0], piece[1]
        two_real = jnp.logical_and(lane < 32, is_first)
        low_real = jnp.where(column < row, both_real, jnp.where(here, 1.0 / both_real, 0.0))
        low_imag = jnp.where(
            column < row, both_imag, jnp.where(jnp.logical_and(here, two_real), 1.0 / both_imag, 0.0)
        )
        good = row < NB
        low_real = jnp.where(good, low_real, 0.0)
        low_imag = jnp.where(good, low_imag, 0.0)
        cross = jnp.where(two_real, 0.0, low_imag)
        own = jnp.where(two_real, low_imag, low_real)
        for s in range(4):
            slot = 4 * group + s

            def spread(value):
                return jnp.take_along_axis(value, 32 * s + column, axis=1, mode="promise_in_bounds")

            wide_cross = spread(cross)
            top = jnp.where(even, spread(low_real), wide_cross)
            bottom = jnp.where(even, -wide_cross, spread(own))
            l0, l1, l2 = (part.astype(jnp.float32) for part in slices_of(jnp.concatenate([top, bottom], axis=0), 3))
            left = [l0, jnp.where(wide, l1, l0), jnp.where(wide, l1, l2)]
            left = jnp.concatenate([part.astype(jnp.bfloat16) for part in left], axis=1)
            r0, r1, r2 = slices_of(jnp.concatenate([spec_ref[slot], spec_ref[SLOTS + slot]], axis=0), 3)
            right = jnp.concatenate([r0, r1, r0, r2, r1, r0], axis=0)
            out = jnp.dot(left, right, preferred_element_type=jnp.float32)
            real, imag = out[:32], out[32:]
            if s == 0:
                last_real = jnp.where(is_first, imag, last_real)
                imag = jnp.where(is_first, 0.0, imag)
            put(slot, real, imag)
    if side == 0:
        last_ref[...] = last_real
    else:
        put(SLOTS, last_real, None)
        last_triangle = jnp.zeros((NB, NB), jnp.float32)
        for c, parts in ((0, others), (1, pieces)):
            for d, piece in enumerate(parts):
                group = group_of(c, d)
                upper_real = jnp.where(column >= row, piece[0], 0.0)
                upper_imag = jnp.where(column >= row, piece[1], 0.0)
                for s in range(4):
                    square = upper_imag[:NB, 32 * s:32 * s + NB]
                    if s == 0:
                        last_triangle = jnp.where(group == 0, square, last_triangle)
                        square = jnp.where(group == 0, 0.0, square)
                    triangle_ref[0, 4 * group + s] = upper_real[:NB, 32 * s:32 * s + NB]
                    triangle_ref[1, 4 * group + s] = square
        triangle_ref[0, SLOTS] = last_triangle
        triangle_ref[1, SLOTS] = jnp.zeros((NB, NB), jnp.float32)
    for copy in copies:
        copy.wait()


def call(body, out_shape, scratch, operands, out_spaces=None, aliases=None):
    vmem = pl.BlockSpec(memory_space=pltpu.VMEM)
    return pl.pallas_call(
        body,
        out_shape=out_shape,
        in_specs=[
            pl.BlockSpec(memory_space=pl.ANY) if number in (aliases or {}) else vmem
            for number in range(len(operands))
        ],
        input_output_aliases=aliases or {},
        out_specs=[pl.BlockSpec(memory_space=space) for space in out_spaces] if out_spaces else jax.tree.map(lambda _: vmem, out_shape),
        scratch_shapes=scratch,
        compiler_params=pltpu.CompilerParams(vmem_limit_bytes=VMEM_BYTES),
    )(*operands)


def f32(*shape):
    return jax.ShapeDtypeStruct(shape, jnp.float32)


def xor_pairs(size, difference):
    return [(i, i ^ difference) for i in range(size)]


def factor_over_devices(spec, got, scale):
    tm, pts = lax.axis_size("tm"), lax.axis_size("pts")
    part = f32(2, 32, 128)
    keep = call(keep_kernel, f32(SIDE - 1, 2, 32, 128), [], [spec])
    parts = call(core_sum_kernel, (part,) * (SIDE - 1), [], [keep, got])
    parts = [lax.ppermute(parts[d - 1], "pts", xor_pairs(pts, d)) for d in range(SIDE - 1, 0, -1)]
    parts = [call(own_kernel, part, [], [spec, got])] + parts
    total = call(pair_sum_kernel, part, [], parts)
    if pts > SIDE:
        parts = [total] + [lax.ppermute(total, "pts", xor_pairs(pts, d)) for d in range(SIDE, pts, SIDE)]
        total = call(pair_sum_kernel, part, [], parts)
    parts = [total] + [lax.ppermute(total, "tm", xor_pairs(tm, d)) for d in range(2, tm, 2)]
    own = call(functools.partial(factor_kernel, scale=scale), part, [], parts)
    own = [own] + [lax.ppermute(own, "pts", xor_pairs(pts, d)) for d in range(1, SIDE)]
    return own + [lax.ppermute(piece, "tm", xor_pairs(tm, 1)) for piece in own]


def shards(snapshots, weights):
    tm, pts = lax.axis_size("tm"), lax.axis_size("pts")
    me = lax.axis_index("tm")
    points = weights.shape[0]
    scale = 1.0 / (points * tm * pts)

    def piece_of(array, d, start, size):
        return lax.dynamic_slice_in_dim(array, (me ^ d) * points + start, size, 1)

    def exchanged(piece, d):
        return lax.ppermute(piece, "tm", xor_pairs(tm, d))

    last = max(128, points // 4 // 128 * 128)
    body = points - last
    parted = {tm // 2 + 1: tm - 1, 3 * tm // 4: tm - 1}
    pieces = {}
    farthest = tm - 1
    sent = piece_of(snapshots, farthest, 0, points)
    rest, sent = lax.optimization_barrier((snapshots, sent))
    pieces[farthest, 0] = exchanged(sent, farthest)
    for d in reversed(range(farthest)):
        piece = piece_of(rest, d, 0, body if d in parted else points)
        pieces[d, 0] = exchanged(piece, d) if d else piece
    for d, after in parted.items():
        sent = piece_of(rest, d, body, last)
        if after is not None:
            sent, _ = lax.optimization_barrier((sent, pieces[after, 0]))
        pieces[d, body] = exchanged(sent, d)
    root = jnp.sqrt(weights)[None, :]
    table_t = jnp.asarray(fourier_table().T)
    half = f32(SIDE, 2, 32, 128)
    spec, send = call(
        functools.partial(spectrum_kernel, places=tuple(pieces)),
        (f32(SEG, 32, points), half),
        [pltpu.VMEM((NT, points), jnp.float32)],
        [table_t, root, *pieces.values()],
    )
    got = lax.ppermute(send, "tm", xor_pairs(tm, 1))
    factors = factor_over_devices(spec, got, scale)
    tiles = points // 128
    shape = f32(NF, NB, tiles * 2, 128)
    scratch = [pltpu.VMEM((4 * SIDE + 1, NB, tiles * 2, 128), jnp.float32), pltpu.SemaphoreType.DMA((4 * SIDE + 1,))]
    own, others = factors[:SIDE], factors[SIDE:]
    modes, last_real = call(
        functools.partial(apply_kernel, side=0),
        (shape, f32(32, points)),
        scratch,
        [*own, spec],
        [pl.ANY, pltpu.VMEM],
    )
    modes, triangle = call(
        functools.partial(apply_kernel, side=1),
        (shape, f32(2, NF, NB, NB)),
        scratch,
        [*others, spec, *own, last_real, modes],
        [pl.ANY, pltpu.VMEM],
        {2 * SIDE + 2: 0},
    )
    modes = modes.reshape(NF, NB, tiles, 2, 128).transpose(3, 0, 1, 2, 4).reshape(2, NF, NB, points)
    return (modes, triangle)


def solution(mesh):
    placed = (P("tm", "pts"), P(("pts", "tm")))
    return jax.shard_map(
        shards,
        mesh=mesh,
        in_specs=placed,
        out_specs=(P(None, None, None, ("pts", "tm")), P()),
        check_vma=False,
    )
```
